1024 devices in a mesh: dp: 16 (over z), node: 4 (over x), local: 16 (over y, core).
Axes of the slice: x: 4, y: 8, z: 16, core: 2. Of those that a mesh axis runs over, the one named last changes fastest.
Arguments:
- tokens: bfloat16 [16384, 7168], P(('dp', 'node'), 'local'), parts along dimension 0, may hold values from -6 to 6
- routes: int32 [16384, 2], P(('dp', 'node')), parts along dimension 0, may hold values from 0 to 3, all different within a row; in each aligned block of 256 rows (0 to 255, 256 to 511, ...) at most 160 rows name the same one
- route_weight: float32 [16384, 2], P(('dp', 'node')), parts along dimension 0, may hold values from 0.1 to 1
- w_gate: bfloat16 [4, 7168, 2048], P('node', None, 'local'), may hold values from -0.0625 to 0.0625
- w_up: bfloat16 [4, 7168, 2048], P('node', None, 'local'), may hold values from -0.0625 to 0.0625
- w_down: bfloat16 [4, 2048, 7168], P('node', None, 'local'), may hold values from -0.125 to 0.125
Outputs:
- mixed: bfloat16 [16384, 7168], P(('dp', 'node'), 'local'), parts along dimension 0
The draws below stay inside these ranges and needn't reach their ends.
There are 16 independent parts, one for each index of `dp`. The reference program is written for one: setup_inputs(seed, part) draws one part's arguments, and reference() takes and returns one part's arrays. A program takes and returns all parts, laid end to end along the dimension named above; an argument that names none is the same for every part. Nothing has to cross between parts.
Inputs may be any that keep to these rules, and one draw needn't show every extreme that they name: `routes`: each token names 2 different experts. Among the 256 tokens of one index of node (aligned blocks of rows) no expert is named more than 160 times, a bound that some block reaches.
All inputs are finite; a program needn't handle non-finite values.
Results may differ from the reference program's by a relative error of at most 0.0057.
Values may be sent and summed in bfloat16 or wider, within the bound.
No kernel may reach another device: no remote copies, remote signals or barrier semaphores. Data moves between devices by JAX's collectives and lax.ppermute only.
A program may use at most 64 MiB of HBM per device.

```python
import math
import jax
import jax.numpy as jnp
import numpy as np

D = 7168
FF = 2048
TOP = 2
TOK_DEV = 256
EXPERTS = 4
CAP = 160
TOKENS = 1024


def shard_levels(own_key, extent, pieces, smallest, top_value):
    def one(position, blocks):
        draws = jax.random.uniform(jax.random.fold_in(jax.random.fold_in(own_key, 6), position), (blocks,), jnp.float32, smallest / len(pieces), top_value / len(pieces))
        return jnp.repeat(jnp.exp(draws), extent[position] // blocks).reshape((-1,) + (1,) * (len(extent) - position - 1))

    level = one(*pieces[0])
    for cut in pieces[1:]:
        level = level * one(*cut)
    return level


def deal_out(stream_key, own, number, rows, number_of, top, bound, slope):
    ranking = jax.random.permutation(stream_key, number_of)
    heavy_load, usual = shares(number_of, rows * top, bound, slope, True), shares(number_of, rows * top, bound, slope, False)
    places = jnp.arange(number_of)

    def named(lengths, rotation):
        used = int((lengths > 0).sum())
        fixed = max(1, used // 4)
        moved = fixed + (places - fixed + rotation * (used - fixed)) % max(1, number_of - fixed)
        return jnp.zeros((number_of,), jnp.int32).at[ranking[jnp.where(places < fixed, places, moved)]].set(jnp.asarray(lengths, jnp.int32))

    lengths = jnp.where(number % 4 == 0, named(heavy_load, number // 4), named(usual, number - number // 4 - 1))
    mixed = jax.random.permutation(jax.random.fold_in(own, 3), number_of)
    donor, receiver = mixed[0:number_of // 2 * 2:2], mixed[1:number_of // 2 * 2:2]
    margin = jnp.minimum(lengths[donor] - 1, bound - lengths[receiver]) // 2
    margin = jnp.where((donor == ranking[0]) | (receiver == ranking[0]) | (lengths[receiver] == 0), 0, jnp.maximum(margin, 0))
    moved = jax.random.randint(jax.random.fold_in(own, 4), (number_of // 2,), 0, 1 << 20) % (margin + 1)
    lengths = lengths.at[donor].add(-moved).at[receiver].add(moved)
    items = jnp.searchsorted(jnp.cumsum(lengths), jnp.arange(rows * top), side="right").astype(jnp.int32)
    table = items.reshape(top, rows).T
    table = table[jax.random.permutation(jax.random.fold_in(own, 1), rows)]
    rotation = jax.random.randint(jax.random.fold_in(own, 2), (rows, 1), 0, top)
    return jnp.take_along_axis(table, (jnp.arange(top)[None, :] + rotation) % top, axis=1)


def shares(amount, total, bound, lean, full):
    weights = [(1 << 20) // math.isqrt(rank ** lean) + 1 for rank in range(1, amount + 1)]
    largest = bound if full else min(bound, max(-(-total // amount), total * weights[0] // sum(weights)))
    least = 1 if total - largest >= amount - 1 else 0
    given, rest = [largest] + [least] * (amount - 1), total - largest - least * (amount - 1)
    while rest > 0:
        free = [i for i in range(1, amount) if given[i] < largest] or [i for i in range(1, amount) if given[i] < bound]
        pool, budget = sum([weights[i] for i in free]), rest
        for i in free:
            extra = min(bound - given[i], max(1, budget * weights[i] // pool), rest)
            given[i] = given[i] + extra
            rest = rest - extra
    return np.array(given)


def normal_values(rng, extent, deviation, limit, shards=(), held_as=jnp.bfloat16):
    array = deviation * jax.random.normal(rng, extent, jnp.float32)
    if shards:
        array = array * shard_levels(rng, extent, shards, -0.22, 0.18)
    return jnp.clip(array, -limit, limit).astype(held_as)


def setup_inputs(seed: int = 0, part: int = 0) -> dict:
    arg_keys = jax.random.split(jax.random.key(seed), 7)
    part_keys = jax.random.split(jax.random.fold_in(arg_keys[6], part), 7)
    tokens = normal_values(part_keys[0], (TOKENS, D), 1.0, 6.0, ((0, 4), (1, 16)))
    routes_keys = jax.random.split(jax.random.fold_in(part_keys[1], 1), TOKENS // TOK_DEV)
    routes_turns = jax.random.permutation(jax.random.fold_in(part_keys[1], 3), TOKENS // TOK_DEV)
    routes = jax.vmap(lambda own, number: deal_out(jax.random.fold_in(part_keys[1], 2), own, number, TOK_DEV, EXPERTS, TOP, CAP, 2))(routes_keys, routes_turns).reshape((TOKENS, TOP))
    route_weight = jnp.clip(jnp.exp(math.log(1.0) - 2.3025851 * jax.random.uniform(part_keys[2], (TOKENS, TOP), jnp.float32) ** shard_levels(part_keys[2], (TOKENS, TOP), ((0, 4),), -0.2, 0.2)), 0.1, 1.0)
    w_gate = normal_values(arg_keys[3], (EXPERTS, D, FF), D ** -0.5, 0.0625, ((0, 4), (2, 16)))
    w_up = normal_values(arg_keys[4], (EXPERTS, D, FF), D ** -0.5, 0.0625, ((0, 4), (2, 16)))
    w_down = normal_values(arg_keys[5], (EXPERTS, FF, D), FF ** -0.5, 0.125, ((0, 4), (2, 16)))
    return {"tokens": tokens, "routes": routes, "route_weight": route_weight, "w_gate": w_gate, "w_up": w_up, "w_down": w_down}


def expert_forward(tokens, gate_w, up_w, down_w):
    gate = jnp.dot(tokens, gate_w, preferred_element_type=jnp.float32)
    up = jnp.dot(tokens, up_w, preferred_element_type=jnp.float32)
    hidden = (jax.nn.silu(gate) * up).astype(jnp.bfloat16)
    return jnp.dot(hidden, down_w, preferred_element_type=jnp.float32).astype(jnp.bfloat16)


def reference(tokens, routes, route_weight, w_gate, w_up, w_down):
    outputs = jnp.stack([expert_forward(tokens, w_gate[e], w_up[e], w_down[e]) for e in range(EXPERTS)])
    row_index = jnp.arange(tokens.shape[0], dtype=jnp.int32)
    total = jnp.zeros(tokens.shape, jnp.float32)
    for k in range(TOP):
        picked = outputs[routes[:, k], row_index].astype(jnp.float32)
        total = total + route_weight[:, k][:, None] * picked
    return total.astype(jnp.bfloat16)
```

```python
import functools

import jax
import jax.numpy as jnp
from jax import lax
from jax.experimental import pallas as pl
from jax.experimental.pallas import tpu as pltpu
from jax.sharding import Mesh, PartitionSpec as P

F32, BF16 = jnp.float32, jnp.bfloat16
SWAP = [(0, 1), (1, 0)]
EARLY = 4
VMEM_LIMIT = 48 * 1024 * 1024
NT = (((1,), (1,)), ((), ()))
TN = (((0,), (0,)), ((), ()))


def dispatch_kernel(core_ref, own_ref, other_ref, routes_ref, late_ref, early_ref, pick_ref, both):
    width, count = own_ref.shape
    nodes, early, _ = early_ref.shape
    late = late_ref.shape[1]
    half = early + late
    core = core_ref[0]
    both[pl.ds(pl.multiple_of(core * width, width), width), :] = own_ref[...]
    both[pl.ds(pl.multiple_of((1 - core) * width, width), width), :] = other_ref[...]
    first, second = routes_ref[0:1, :], routes_ref[1:2, :]
    experts = lax.broadcasted_iota(jnp.int32, (8, count), 0)
    member = (first == experts) | (second == experts)
    before = lax.broadcasted_iota(jnp.int32, (count, count), 0)
    after = lax.broadcasted_iota(jnp.int32, (count, count), 1)
    slots = jnp.dot(
        member.astype(F32).astype(BF16),
        (before < after).astype(F32).astype(BF16),
        preferred_element_type=F32,
    ).astype(jnp.int32)
    for k, route in enumerate((first, second)):
        slot = jnp.sum(jnp.where(route == experts, slots, 0), axis=0, keepdims=True)
        pick_ref[k : k + 1, :] = route * (2 * half) + slot
    wanted = lax.broadcasted_iota(jnp.int32, (half, count), 0) + core * half
    for e in range(nodes):
        chosen = (first == e) | (second == e)
        place = jnp.where(chosen, slots[e : e + 1, :], -1)
        picker = (wanted == place).astype(F32).astype(BF16)
        rows = lax.dot_general(picker, both[...], NT, preferred_element_type=F32).astype(BF16)
        early_ref[e] = rows[:early]
        late_ref[e] = rows[early:]


def dispatch(core, own, other, routes, nodes, early, late):
    width, count = own.shape
    return pl.pallas_call(
        dispatch_kernel,
        out_shape=(
            jax.ShapeDtypeStruct((nodes, late, 2 * width), BF16),
            jax.ShapeDtypeStruct((nodes, early, 2 * width), BF16),
            jax.ShapeDtypeStruct((2, count), jnp.int32),
        ),
        in_specs=[pl.BlockSpec(memory_space=pltpu.SMEM)] + [pl.BlockSpec(memory_space=pltpu.VMEM)] * 3,
        out_specs=(pl.BlockSpec(memory_space=pltpu.VMEM),) * 3,
        scratch_shapes=[pltpu.VMEM((2 * width, count), BF16)],
        compiler_params=pltpu.CompilerParams(vmem_limit_bytes=VMEM_LIMIT),
        cost_estimate=pl.CostEstimate(flops=4 * nodes * (early + late) * count * width, bytes_accessed=2000000, transcendentals=0),
    )(core, own, other, routes)


def form_hidden(value, core, out, at):
    size, hid = value.shape[0], value.shape[1] // 4
    gate, up = value[:, :hid], value[:, hid : 2 * hid]
    own = gate / (1.0 + jnp.exp(-gate)) * up
    gate, up = value[:, 2 * hid : 3 * hid], value[:, 3 * hid :]
    other = gate / (1.0 + jnp.exp(-gate)) * up
    left = jnp.where(core == 0, own, other).astype(BF16)
    right = jnp.where(core == 0, other, own).astype(BF16)
    for k in range(out.shape[0]):
        out[k, at : at + size, :hid] = left
        out[k, at : at + size, hid:] = right


def gathered_kernel(core_ref, rows_ref, *refs):
    weights, out, total = refs[:4], refs[4], refs[5]
    k = pl.program_id(0)
    w = jnp.concatenate([ref[...] for ref in weights], axis=1)
    part = jnp.dot(rows_ref[0], w, preferred_element_type=F32)

    @pl.when(k == 0)
    def _():
        total[...] = part

    @pl.when(k > 0)
    def _():
        total[...] += part

    @pl.when(k == pl.num_programs(0) - 1)
    def _():
        form_hidden(total[...], core_ref[0], out, 0)


def gathered_gate_up(core, rows, weights):
    chips, size, width = rows.shape
    hid = weights[0].shape[1]
    return pl.pallas_call(
        gathered_kernel,
        grid=(chips,),
        out_shape=jax.ShapeDtypeStruct((chips, size, 2 * hid), BF16),
        in_specs=[pl.BlockSpec(memory_space=pltpu.SMEM), pl.BlockSpec((1, size, width), lambda k: (k, 0, 0))]
        + [pl.BlockSpec((width, hid), lambda k: (k, 0))] * 4,
        out_specs=pl.BlockSpec((chips, size, 2 * hid), lambda k: (0, 0, 0)),
        scratch_shapes=[pltpu.VMEM((size, 4 * hid), F32)],
        compiler_params=pltpu.CompilerParams(vmem_limit_bytes=VMEM_LIMIT),
        cost_estimate=pl.CostEstimate(
            flops=2 * chips * size * width * 4 * hid, bytes_accessed=2 * chips * width * (size + 4 * hid), transcendentals=0
        ),
    )(core, rows, *weights)


def gate_up_kernel(layout, acc_in, last, idx_ref, *refs):
    count = len(layout)
    blocks, weights = refs[:count], refs[count : 5 * count]
    sums = refs[5 * count : 5 * count + len(acc_in)]
    outs = refs[5 * count + len(acc_in) :]
    total = [s[...] for s in sums] if acc_in else [None] * (1 + max(c for c, _ in layout))
    for j, (chain, at) in enumerate(layout):
        w = jnp.concatenate([ref[...] for ref in weights[4 * j : 4 * j + 4]], axis=1)
        part = jnp.dot(blocks[j][...], w, preferred_element_type=F32)
        if total[chain] is None:
            total[chain] = part
        elif part.shape == total[chain].shape:
            total[chain] = total[chain] + part
        else:
            size = part.shape[0]
            pieces = [total[chain][:at], total[chain][at : at + size] + part, total[chain][at + size :]]
            total[chain] = jnp.concatenate([p for p in pieces if p.shape[0]], axis=0)
    if not last:
        for out, value in zip(outs, total):
            out[...] = value
        return
    at = 0
    for value in total:
        form_hidden(value, idx_ref[idx_ref.shape[0] - 1], outs[0], at)
        at += value.shape[0]


def gate_up(items, sums, weights, idx, last=None):
    layout = tuple((c, at) for c, at, _, _ in items)
    blocks = [b for _, _, b, _ in items]
    width, hid = blocks[0].shape[1], weights[0].shape[1]
    whole = lambda shape: pl.BlockSpec(shape, lambda i, idx: (0,) * len(shape))
    in_specs = [whole(b.shape) for b in blocks]
    operands = list(blocks)
    for j in range(len(items)):
        for w in weights:
            in_specs.append(pl.BlockSpec((width, hid), functools.partial(lambda at, i, idx: (idx[at], 0), items[j][3])))
            operands.append(w)
    first_sum = 1 + len(operands)
    for s in sums:
        in_specs.append(whole(s.shape))
        operands.append(s)
    if last is not None:
        shapes = [jax.ShapeDtypeStruct(last, BF16)]
        aliases = {}
    elif sums:
        shapes = [jax.ShapeDtypeStruct(s.shape, F32) for s in sums]
        aliases = {first_sum + k: k for k in range(len(sums))}
    else:
        sizes = {}
        for c, _, b, _ in items:
            sizes[c] = b.shape[0]
        shapes = [jax.ShapeDtypeStruct((sizes[c], 4 * hid), F32) for c in sorted(sizes)]
        aliases = {}
    rows = sum(b.shape[0] for b in blocks)
    return pl.pallas_call(
        functools.partial(gate_up_kernel, layout, tuple(s.shape for s in sums), last is not None),
        grid_spec=pltpu.PrefetchScalarGridSpec(
            num_scalar_prefetch=1,
            grid=(1,),
            in_specs=in_specs,
            out_specs=[whole(s.shape) for s in shapes],
        ),
        out_shape=shapes,
        input_output_aliases=aliases,
        compiler_params=pltpu.CompilerParams(vmem_limit_bytes=VMEM_LIMIT),
        cost_estimate=pl.CostEstimate(
            flops=2 * rows * width * 4 * hid, bytes_accessed=len(items) * 4 * width * hid * 2 + 4 * rows * width, transcendentals=0
        ),
    )(idx, *operands)


def down_kernel(core_ref, early_ref, late_ref, own_ref, other_ref, out_ref, early_sums, late_sums):
    k = pl.program_id(0)
    nodes, _, half, _ = out_ref.shape
    core = core_ref[0]
    for hidden_ref, sums in ((early_ref, early_sums), (late_ref, late_sums)):
        for j, ref in enumerate((own_ref, other_ref)):
            part = lax.dot_general(hidden_ref[0], ref[...], NT, preferred_element_type=F32)

            @pl.when(k == 0)
            def _():
                sums[j] = part

            @pl.when(k > 0)
            def _():
                sums[j] += part

    @pl.when(k == pl.num_programs(0) - 1)
    def _():
        at = 0
        for sums in (early_sums, late_sums):
            size = sums.shape[1] // nodes
            for e in range(nodes):
                rows = slice(e * size, (e + 1) * size)
                out_ref[e, core, at : at + size] = sums[0, rows, :].astype(BF16)
                out_ref[e, 1 - core, at : at + size] = sums[1, rows, :].astype(BF16)
            at += size


def down(core, early, late, own, other, nodes):
    chips, _, depth = early.shape
    width = own.shape[0]
    rows = early.shape[1] + late.shape[1]
    half = rows // nodes
    return pl.pallas_call(
        down_kernel,
        grid=(chips,),
        out_shape=jax.ShapeDtypeStruct((nodes, 2, half, width), BF16),
        in_specs=[
            pl.BlockSpec(memory_space=pltpu.SMEM),
            pl.BlockSpec((1,) + early.shape[1:], lambda k: (k, 0, 0)),
            pl.BlockSpec((1,) + late.shape[1:], lambda k: (k, 0, 0)),
            pl.BlockSpec((width, depth), lambda k: (0, k)),
            pl.BlockSpec((width, depth), lambda k: (0, k)),
        ],
        out_specs=pl.BlockSpec((nodes, 2, half, width), lambda k: (0, 0, 0, 0)),
        scratch_shapes=[pltpu.VMEM((2, early.shape[1], width), F32), pltpu.VMEM((2, late.shape[1], width), F32)],
        compiler_params=pltpu.CompilerParams(vmem_limit_bytes=VMEM_LIMIT),
        cost_estimate=pl.CostEstimate(flops=4 * rows * depth * chips * width, bytes_accessed=6000000, transcendentals=0),
    )(core, early, late, own, other)


def combine_kernel(rows_ref, pick_ref, weight_ref, out_ref):
    total = rows_ref.shape[0]
    count = pick_ref.shape[1]
    row = lax.broadcasted_iota(jnp.int32, (total, count), 0)
    scale = jnp.zeros((total, count), F32)
    for k in range(pick_ref.shape[0]):
        scale = jnp.where(row == pick_ref[k : k + 1, :], weight_ref[k : k + 1, :], scale)
    high = scale.astype(BF16)
    low = (scale - high.astype(F32)).astype(BF16)
    rows = rows_ref[...]
    mixed = lax.dot_general(rows, high, TN, preferred_element_type=F32)
    mixed = mixed + lax.dot_general(rows, low, TN, preferred_element_type=F32)
    out_ref[...] = mixed.astype(BF16)


def combine(rows, pick, weight):
    total, width = rows.shape
    count = pick.shape[1]
    return pl.pallas_call(
        combine_kernel,
        out_shape=jax.ShapeDtypeStruct((width, count), BF16),
        in_specs=[pl.BlockSpec(memory_space=pltpu.VMEM)] * 3,
        out_specs=pl.BlockSpec(memory_space=pltpu.VMEM),
        compiler_params=pltpu.CompilerParams(vmem_limit_bytes=VMEM_LIMIT),
        cost_estimate=pl.CostEstimate(flops=4 * total * count * width, bytes_accessed=1500000, transcendentals=0),
    )(rows, pick, weight)


def local(tokens, routes, route_weight, w_gate, w_up, w_down):
    nodes, chips = lax.axis_size("node"), lax.axis_size("y")
    count, width = tokens.shape
    capacity = min(count, 5 * count * routes.shape[1] // (4 * nodes))
    half = capacity // 2
    early = half * EARLY // 10
    late = half - early
    core, here = lax.axis_index("core"), lax.axis_index("y")
    core1 = core.astype(jnp.int32)[None]
    idx = jnp.concatenate([lax.rem(here + jnp.arange(chips), chips).astype(jnp.int32), core1])

    def hop(x, distance):
        return lax.ppermute(x, "y", [(i, (i + distance) % chips) for i in range(chips)])

    def across(x):
        return lax.ppermute(x, "core", SWAP)

    def exchange(x, axes):
        return lax.all_to_all(x, axes, split_axis=0, concat_axis=0, tiled=True)

    own = tokens.T
    late_rows, early_rows, pick = dispatch(core1, own, across(own), routes.T, nodes, early, late)
    late_rows = exchange(late_rows, "node")
    early_rows, late_rows = lax.optimization_barrier((early_rows, late_rows))
    late_all = lax.all_gather(late_rows.reshape(nodes * late, 2 * width), "y", axis=0)
    early_rows = exchange(early_rows, "node").reshape(nodes * early, 2 * width)

    gate_w, up_w, down_w = w_gate[0], w_up[0], w_down[0].T
    size = nodes * early
    up_y, down_y = hop(early_rows, 1), hop(early_rows, -1)
    gate_w, up_w, down_w, up_y, down_y = lax.optimization_barrier((gate_w, up_w, down_w, up_y, down_y))
    weights = (gate_w, up_w, across(gate_w), across(up_w))
    sums = gate_up([(0, 0, early_rows, 0), (0, 0, up_y, chips - 1), (0, 0, down_y, 1)], [], weights, idx)
    for s in range(2, chips // 2):
        up_y, down_y = hop(up_y, 1), hop(down_y, -1)
        new = gate_up([(0, 0, up_y, chips - s), (0, 0, down_y, s)], sums, weights, idx)
        if s < chips // 2 - 1:
            up_y, down_y, down_w, *sums = lax.optimization_barrier((up_y, down_y, down_w, *sums))
        sums = new
    far = chips // 2
    items = [(0, 0, hop(up_y[: size // 2], 1), far), (0, size // 2, hop(down_y[size // 2 :], -1), far)]
    down_other = across(down_w)
    early_hidden = gate_up(items, sums, weights, idx, last=(chips, size, 2 * gate_w.shape[1]))[0]
    early_hidden = exchange(early_hidden, "y")
    late_hidden = exchange(gathered_gate_up(core1, late_all, weights), "y")
    out = down(core1, early_hidden, late_hidden, down_w, down_other, nodes)
    back = exchange(out.reshape(2 * nodes, half, width), ("node", "core"))
    return combine(back.reshape(2 * nodes * half, width), pick, route_weight.T).T


def solution(mesh):
    shape = mesh.devices.shape
    split = Mesh(mesh.devices.reshape(shape[:2] + (shape[2] // 2, 2)), ("dp", "node", "y", "core"))
    rows, cols = ("dp", "node"), ("y", "core")
    return jax.shard_map(
        local,
        mesh=split,
        in_specs=(
            P(rows, cols),
            P(rows, None),
            P(rows, None),
            P("node", None, cols),
            P("node", None, cols),
            P("node", None, cols),
        ),
        out_specs=P(rows, cols),
        check_vma=False,
    )
```

```python
import jax
import jax.numpy as jnp
from jax import lax
from jax.experimental import pallas as pl
from jax.experimental.pallas import tpu as pltpu
from jax.sharding import Mesh, PartitionSpec as P

F32, BF16 = jnp.float32, jnp.bfloat16
SWAP = [(0, 1), (1, 0)]
EARLY = 4
VMEM_LIMIT = 52 * 1024 * 1024
NT = (((1,), (1,)), ((), ()))
TN = (((0,), (0,)), ((), ()))


def whole(shape):
    return pl.BlockSpec(shape, lambda i: (0,) * len(shape))


def dispatch_kernel(core_ref, own_ref, other_ref, routes_ref, late_ref, early_ref, pick_ref, both):
    width, count = own_ref.shape
    nodes, early, _ = early_ref.shape
    late = late_ref.shape[1]
    half = early + late
    core = core_ref[0]
    both[pl.ds(pl.multiple_of(core * width, width), width), :] = own_ref[...]
    both[pl.ds(pl.multiple_of((1 - core) * width, width), width), :] = other_ref[...]
    first, second = routes_ref[0:1, :], routes_ref[1:2, :]
    experts = lax.broadcasted_iota(jnp.int32, (8, count), 0)
    member = (first == experts) | (second == experts)
    before = lax.broadcasted_iota(jnp.int32, (count, count), 0)
    after = lax.broadcasted_iota(jnp.int32, (count, count), 1)
    slots = jnp.dot(
        member.astype(F32).astype(BF16),
        (before < after).astype(F32).astype(BF16),
        preferred_element_type=F32,
    ).astype(jnp.int32)
    for k, route in enumerate((first, second)):
        slot = jnp.sum(jnp.where(route == experts, slots, 0), axis=0, keepdims=True)
        pick_ref[k : k + 1, :] = route * (2 * half) + slot
    wanted = lax.broadcasted_iota(jnp.int32, (half, count), 0) + core * half
    for e in range(nodes):
        chosen = (first == e) | (second == e)
        place = jnp.where(chosen, slots[e : e + 1, :], -1)
        picker = (wanted == place).astype(F32).astype(BF16)
        rows = lax.dot_general(picker, both[...], NT, preferred_element_type=F32).astype(BF16)
        early_ref[e] = rows[:early]
        late_ref[e] = rows[early:]


def dispatch(core, own, other, routes, nodes, early, late):
    width, count = own.shape
    return pl.pallas_call(
        dispatch_kernel,
        out_shape=(
            jax.ShapeDtypeStruct((nodes, late, 2 * width), BF16),
            jax.ShapeDtypeStruct((nodes, early, 2 * width), BF16),
            jax.ShapeDtypeStruct((2, count), jnp.int32),
        ),
        grid=(1,),
        in_specs=[pl.BlockSpec(memory_space=pltpu.SMEM)] + [whole(x.shape) for x in (own, other, routes)],
        out_specs=(
            whole((nodes, late, 2 * width)),
            whole((nodes, early, 2 * width)),
            whole((2, count)),
        ),
        scratch_shapes=[pltpu.VMEM((2 * width, count), BF16)],
        compiler_params=pltpu.CompilerParams(vmem_limit_bytes=VMEM_LIMIT),
        cost_estimate=pl.CostEstimate(flops=4 * nodes * (early + late) * count * width, bytes_accessed=2000000, transcendentals=0),
    )(core, own, other, routes)


def form_hidden(value, core, out, at):
    size, hid = value.shape[0], value.shape[1] // 4
    gate, up = value[:, :hid], value[:, hid : 2 * hid]
    own = gate / (1.0 + jnp.exp(-gate)) * up
    gate, up = value[:, 2 * hid : 3 * hid], value[:, 3 * hid :]
    other = gate / (1.0 + jnp.exp(-gate)) * up
    left = jnp.where(core == 0, own, other).astype(BF16)
    right = jnp.where(core == 0, other, own).astype(BF16)
    for k in range(out.shape[0]):
        out[k, at : at + size, :hid] = left
        out[k, at : at + size, hid:] = right


def gate_up_kernel(core_ref, rows_ref, *refs):
    weights, out, total = refs[:4], refs[4], refs[5]
    k = pl.program_id(0)
    chips, _, width = rows_ref.shape
    part = None
    for j in range(chips):
        w = jnp.concatenate([ref[j * width : (j + 1) * width, :] for ref in weights], axis=1)
        term = jnp.dot(rows_ref[j], w, preferred_element_type=F32)
        part = term if part is None else part + term

    @pl.when(k == 0)
    def _():
        total[...] = part

    @pl.when(k > 0)
    def _():
        total[...] += part

    @pl.when(k == pl.num_programs(0) - 1)
    def _():
        hid = weights[0].shape[1]
        value = total[...]
        gate, up = value[:, :hid], value[:, hid : 2 * hid]
        own = gate / (1.0 + jnp.exp(-gate)) * up
        gate, up = value[:, 2 * hid : 3 * hid], value[:, 3 * hid :]
        other = gate / (1.0 + jnp.exp(-gate)) * up
        left = jnp.where(core_ref[0] == 0, own, other).astype(BF16)
        right = jnp.where(core_ref[0] == 0, other, own).astype(BF16)
        for c in range(out.shape[0]):
            out[c, :, :hid] = left
            out[c, :, hid:] = right


def gate_up(core, rows, weights):
    chips, size, width = rows.shape
    hid = weights[0].shape[1]
    step = 2
    return pl.pallas_call(
        gate_up_kernel,
        grid=(chips // step,),
        out_shape=jax.ShapeDtypeStruct((chips, size, 2 * hid), BF16),
        in_specs=[pl.BlockSpec(memory_space=pltpu.SMEM), pl.BlockSpec((step, size, width), lambda k: (k, 0, 0))]
        + [pl.BlockSpec((step * width, hid), lambda k: (k, 0))] * 4,
        out_specs=pl.BlockSpec((chips, size, 2 * hid), lambda k: (0, 0, 0)),
        scratch_shapes=[pltpu.VMEM((size, 4 * hid), F32)],
        compiler_params=pltpu.CompilerParams(vmem_limit_bytes=VMEM_LIMIT),
        cost_estimate=pl.CostEstimate(
            flops=2 * chips * size * width * 4 * hid, bytes_accessed=2 * chips * width * (size + 4 * hid), transcendentals=0
        ),
    )(core, rows, *weights)


def down_kernel(core_ref, early_ref, late_ref, own_ref, other_ref, out_ref, total):
    k = pl.program_id(0)
    chips, early, depth = early_ref.shape
    part = None
    for j in range(chips):
        hidden = jnp.concatenate([early_ref[j], late_ref[j]], axis=0)
        w = jnp.concatenate([ref[:, j * depth : (j + 1) * depth] for ref in (own_ref, other_ref)], axis=0)
        term = lax.dot_general(hidden, w, NT, preferred_element_type=F32)
        part = term if part is None else part + term

    @pl.when(k == 0)
    def _():
        total[...] = part

    @pl.when(k > 0)
    def _():
        total[...] += part

    @pl.when(k == pl.num_programs(0) - 1)
    def _():
        nodes, _, half, width = out_ref.shape
        core = core_ref[0]
        first = early // nodes
        rest = half - first
        for side, at in ((core, 0), (1 - core, width)):
            for e in range(nodes):
                cut = total[e * first : (e + 1) * first, at : at + width]
                out_ref[e, side, :first] = cut.astype(BF16)
                cut = total[early + e * rest : early + (e + 1) * rest, at : at + width]
                out_ref[e, side, first:] = cut.astype(BF16)


def down(core, early, late, own, other, nodes):
    chips, _, depth = early.shape
    width = own.shape[0]
    rows = early.shape[1] + late.shape[1]
    half = rows // nodes
    step = 2
    return pl.pallas_call(
        down_kernel,
        grid=(chips // step,),
        out_shape=jax.ShapeDtypeStruct((nodes, 2, half, width), BF16),
        in_specs=[
            pl.BlockSpec(memory_space=pltpu.SMEM),
            pl.BlockSpec((step,) + early.shape[1:], lambda k: (k, 0, 0)),
            pl.BlockSpec((step,) + late.shape[1:], lambda k: (k, 0, 0)),
            pl.BlockSpec((width, step * depth), lambda k: (0, k)),
            pl.BlockSpec((width, step * depth), lambda k: (0, k)),
        ],
        out_specs=pl.BlockSpec((nodes, 2, half, width), lambda k: (0, 0, 0, 0)),
        scratch_shapes=[pltpu.VMEM((rows, 2 * width), F32)],
        compiler_params=pltpu.CompilerParams(vmem_limit_bytes=VMEM_LIMIT),
        cost_estimate=pl.CostEstimate(flops=4 * rows * depth * chips * width, bytes_accessed=6000000, transcendentals=0),
    )(core, early, late, own, other)


def combine_kernel(rows_ref, pick_ref, weight_ref, out_ref):
    total = rows_ref.shape[0]
    count = pick_ref.shape[1]
    row = lax.broadcasted_iota(jnp.int32, (total, count), 0)
    scale = jnp.zeros((total, count), F32)
    for k in range(pick_ref.shape[0]):
        scale = jnp.where(row == pick_ref[k : k + 1, :], weight_ref[k : k + 1, :], scale)
    high = scale.astype(BF16)
    low = (scale - high.astype(F32)).astype(BF16)
    rows = rows_ref[...]
    mixed = lax.dot_general(rows, high, TN, preferred_element_type=F32)
    mixed = mixed + lax.dot_general(rows, low, TN, preferred_element_type=F32)
    out_ref[...] = mixed.astype(BF16)


def combine(rows, pick, weight):
    total, width = rows.shape
    count = pick.shape[1]
    return pl.pallas_call(
        combine_kernel,
        out_shape=jax.ShapeDtypeStruct((width, count), BF16),
        grid=(1,),
        in_specs=[whole(x.shape) for x in (rows, pick, weight)],
        out_specs=whole((width, count)),
        compiler_params=pltpu.CompilerParams(vmem_limit_bytes=VMEM_LIMIT),
        cost_estimate=pl.CostEstimate(flops=4 * total * count * width, bytes_accessed=1500000, transcendentals=0),
    )(rows, pick, weight)


def local(tokens, routes, route_weight, w_gate, w_up, w_down):
    nodes, chips = lax.axis_size("node"), lax.axis_size("y")
    count, width = tokens.shape
    capacity = min(count, 5 * count * routes.shape[1] // (4 * nodes))
    half = capacity // 2
    early = half * EARLY // 10
    late = half - early
    core = lax.axis_index("core").astype(jnp.int32)[None]

    def across(x):
        return lax.ppermute(x, "core", SWAP)

    def exchange(x, axes):
        return lax.all_to_all(x, axes, split_axis=0, concat_axis=0, tiled=True)

    own = tokens.T
    late_rows, early_rows, pick = dispatch(core, own, across(own), routes.T, nodes, early, late)
    late_rows = exchange(late_rows, "node")
    early_rows, late_rows = lax.optimization_barrier((early_rows, late_rows))
    late_all = lax.all_gather(late_rows.reshape(nodes * late, 2 * width), "y", axis=0)
    early_rows = exchange(early_rows, "node").reshape(nodes * early, 2 * width)

    gate_w, up_w, down_w = w_gate[0], w_up[0], w_down[0].T
    gate_w, up_w, down_w, early_rows = lax.optimization_barrier((gate_w, up_w, down_w, early_rows))
    early_all = exchange(jnp.broadcast_to(early_rows[None], (chips,) + early_rows.shape), "y")
    weights = (gate_w, up_w, across(gate_w), across(up_w))
    down_other = across(down_w)
    early_hidden = exchange(gate_up(core, early_all, weights), "y")
    late_hidden = exchange(gate_up(core, late_all, weights), "y")
    out = down(core, early_hidden, late_hidden, down_w, down_other, nodes)
    back = exchange(out.reshape(2 * nodes, half, width), ("node", "core"))
    return combine(back.reshape(2 * nodes * half, width), pick, route_weight.T).T


def solution(mesh):
    shape = mesh.devices.shape
    split = Mesh(mesh.devices.reshape(shape[:2] + (shape[2] // 2, 2)), ("dp", "node", "y", "core"))
    rows, cols = ("dp", "node"), ("y", "core")
    return jax.shard_map(
        local,
        mesh=split,
        in_specs=(
            P(rows, cols),
            P(rows, None),
            P(rows, None),
            P("node", None, cols),
            P("node", None, cols),
            P("node", None, cols),
        ),
        out_specs=P(rows, cols),
        check_vma=False,
    )
```

```python
import functools

import jax
import jax.numpy as jnp
from jax import lax
from jax.experimental import pallas as pl
from jax.experimental.pallas import tpu as pltpu
from jax.sharding import Mesh, PartitionSpec as P

F32, BF16 = jnp.float32, jnp.bfloat16
SWAP = [(0, 1), (1, 0)]
VMEM_LIMIT = 52 * 1024 * 1024
NT = (((1,), (1,)), ((), ()))
TN = (((0,), (0,)), ((), ()))


def whole(shape):
    return pl.BlockSpec(shape, lambda i: (0,) * len(shape))


def dispatch_kernel(core_ref, own_ref, other_ref, routes_ref, rows_ref, pick_ref, both):
    width, count = own_ref.shape
    nodes, half, _ = rows_ref.shape
    core = core_ref[0]
    both[pl.ds(pl.multiple_of(core * width, width), width), :] = own_ref[...]
    both[pl.ds(pl.multiple_of((1 - core) * width, width), width), :] = other_ref[...]
    first, second = routes_ref[0:1, :], routes_ref[1:2, :]
    experts = lax.broadcasted_iota(jnp.int32, (8, count), 0)
    member = (first == experts) | (second == experts)
    before = lax.broadcasted_iota(jnp.int32, (count, count), 0)
    after = lax.broadcasted_iota(jnp.int32, (count, count), 1)
    slots = jnp.dot(
        member.astype(F32).astype(BF16),
        (before < after).astype(F32).astype(BF16),
        preferred_element_type=F32,
    ).astype(jnp.int32)
    for k, route in enumerate((first, second)):
        slot = jnp.sum(jnp.where(route == experts, slots, 0), axis=0, keepdims=True)
        pick_ref[k : k + 1, :] = route * (2 * half) + slot
    wanted = lax.broadcasted_iota(jnp.int32, (half, count), 0) + core * half
    for e in range(nodes):
        chosen = (first == e) | (second == e)
        place = jnp.where(chosen, slots[e : e + 1, :], -1)
        picker = (wanted == place).astype(F32).astype(BF16)
        rows_ref[e] = lax.dot_general(picker, both[...], NT, preferred_element_type=F32).astype(BF16)


def dispatch(core, own, other, routes, nodes, half):
    width, count = own.shape
    return pl.pallas_call(
        dispatch_kernel,
        out_shape=(
            jax.ShapeDtypeStruct((nodes, half, 2 * width), BF16),
            jax.ShapeDtypeStruct((2, count), jnp.int32),
        ),
        grid=(1,),
        in_specs=[pl.BlockSpec(memory_space=pltpu.SMEM)] + [whole(x.shape) for x in (own, other, routes)],
        out_specs=(whole((nodes, half, 2 * width)), whole((2, count))),
        scratch_shapes=[pltpu.VMEM((2 * width, count), BF16)],
        compiler_params=pltpu.CompilerParams(vmem_limit_bytes=VMEM_LIMIT),
        cost_estimate=pl.CostEstimate(flops=2 * nodes * half * count * 2 * width, bytes_accessed=2000000, transcendentals=0),
    )(core, own, other, routes)


def form_hidden(value, core, out, at):
    size, hid = value.shape[0], value.shape[1] // 4
    gate, up = value[:, :hid], value[:, hid : 2 * hid]
    own = gate / (1.0 + jnp.exp(-gate)) * up
    gate, up = value[:, 2 * hid : 3 * hid], value[:, 3 * hid :]
    other = gate / (1.0 + jnp.exp(-gate)) * up
    left = jnp.where(core == 0, own, other).astype(BF16)
    right = jnp.where(core == 0, other, own).astype(BF16)
    for k in range(out.shape[0]):
        out[k, at : at + size, :hid] = left
        out[k, at : at + size, hid:] = right


def gate_up_kernel(layout, acc_in, last, idx_ref, *refs):
    count = len(layout)
    blocks, weights = refs[:count], refs[count : 5 * count]
    sums = refs[5 * count : 5 * count + len(acc_in)]
    outs = refs[5 * count + len(acc_in) :]
    total = [s[...] for s in sums] if acc_in else [None] * (1 + max(c for c, _ in layout))
    for j, (chain, at) in enumerate(layout):
        w = jnp.concatenate([ref[...] for ref in weights[4 * j : 4 * j + 4]], axis=1)
        part = jnp.dot(blocks[j][...], w, preferred_element_type=F32)
        if total[chain] is None:
            total[chain] = part
        elif part.shape == total[chain].shape:
            total[chain] = total[chain] + part
        else:
            size = part.shape[0]
            pieces = [total[chain][:at], total[chain][at : at + size] + part, total[chain][at + size :]]
            total[chain] = jnp.concatenate([p for p in pieces if p.shape[0]], axis=0)
    if not last:
        for out, value in zip(outs, total):
            out[...] = value
        return
    at = 0
    for value in total:
        form_hidden(value, idx_ref[idx_ref.shape[0] - 1], outs[0], at)
        at += value.shape[0]


def gate_up(items, sums, weights, idx, last=None):
    layout = tuple((c, at) for c, at, _, _ in items)
    blocks = [b for _, _, b, _ in items]
    width, hid = blocks[0].shape[1], weights[0].shape[1]
    full = lambda shape: pl.BlockSpec(shape, lambda i, idx: (0,) * len(shape))
    in_specs = [full(b.shape) for b in blocks]
    operands = list(blocks)
    for j in range(len(items)):
        for w in weights:
            in_specs.append(pl.BlockSpec((width, hid), functools.partial(lambda at, i, idx: (idx[at], 0), items[j][3])))
            operands.append(w)
    first_sum = 1 + len(operands)
    for s in sums:
        in_specs.append(full(s.shape))
        operands.append(s)
    if last is not None:
        shapes = [jax.ShapeDtypeStruct(last, BF16)]
        aliases = {}
    elif sums:
        shapes = [jax.ShapeDtypeStruct(s.shape, F32) for s in sums]
        aliases = {first_sum + k: k for k in range(len(sums))}
    else:
        sizes = {}
        for c, _, b, _ in items:
            sizes[c] = b.shape[0]
        shapes = [jax.ShapeDtypeStruct((sizes[c], 4 * hid), F32) for c in sorted(sizes)]
        aliases = {}
    rows = sum(b.shape[0] for b in blocks)
    return pl.pallas_call(
        functools.partial(gate_up_kernel, layout, tuple(s.shape for s in sums), last is not None),
        grid_spec=pltpu.PrefetchScalarGridSpec(
            num_scalar_prefetch=1,
            grid=(1,),
            in_specs=in_specs,
            out_specs=[full(s.shape) for s in shapes],
        ),
        out_shape=shapes,
        input_output_aliases=aliases,
        compiler_params=pltpu.CompilerParams(vmem_limit_bytes=VMEM_LIMIT),
        cost_estimate=pl.CostEstimate(
            flops=2 * rows * width * 4 * hid, bytes_accessed=len(items) * 4 * width * hid * 2 + 4 * rows * width, transcendentals=0
        ),
    )(idx, *operands)


def down_kernel(core_ref, hidden_ref, own_ref, other_ref, out_ref, total):
    k = pl.program_id(0)
    chips, _, depth = hidden_ref.shape
    part = None
    for j in range(chips):
        w = jnp.concatenate([ref[:, j * depth : (j + 1) * depth] for ref in (own_ref, other_ref)], axis=0)
        term = lax.dot_general(hidden_ref[j], w, NT, preferred_element_type=F32)
        part = term if part is None else part + term

    @pl.when(k == 0)
    def _():
        total[...] = part

    @pl.when(k > 0)
    def _():
        total[...] += part

    @pl.when(k == pl.num_programs(0) - 1)
    def _():
        nodes, _, half, width = out_ref.shape
        core = core_ref[0]
        for side, at in ((core, 0), (1 - core, width)):
            for e in range(nodes):
                out_ref[e, side] = total[e * half : (e + 1) * half, at : at + width].astype(BF16)


def down(core, hidden, own, other, nodes):
    chips, rows, depth = hidden.shape
    width = own.shape[0]
    half = rows // nodes
    step = 2
    return pl.pallas_call(
        down_kernel,
        grid=(chips // step,),
        out_shape=jax.ShapeDtypeStruct((nodes, 2, half, width), BF16),
        in_specs=[
            pl.BlockSpec(memory_space=pltpu.SMEM),
            pl.BlockSpec((step, rows, depth), lambda k: (k, 0, 0)),
            pl.BlockSpec((width, step * depth), lambda k: (0, k)),
            pl.BlockSpec((width, step * depth), lambda k: (0, k)),
        ],
        out_specs=pl.BlockSpec((nodes, 2, half, width), lambda k: (0, 0, 0, 0)),
        scratch_shapes=[pltpu.VMEM((rows, 2 * width), F32)],
        compiler_params=pltpu.CompilerParams(vmem_limit_bytes=VMEM_LIMIT),
        cost_estimate=pl.CostEstimate(flops=4 * rows * depth * chips * width, bytes_accessed=6000000, transcendentals=0),
    )(core, hidden, own, other)


def combine_kernel(rows_ref, pick_ref, weight_ref, out_ref):
    total = rows_ref.shape[0]
    count = pick_ref.shape[1]
    row = lax.broadcasted_iota(jnp.int32, (total, count), 0)
    scale = jnp.zeros((total, count), F32)
    for k in range(pick_ref.shape[0]):
        scale = jnp.where(row == pick_ref[k : k + 1, :], weight_ref[k : k + 1, :], scale)
    high = scale.astype(BF16)
    low = (scale - high.astype(F32)).astype(BF16)
    rows = rows_ref[...]
    mixed = lax.dot_general(rows, high, TN, preferred_element_type=F32)
    mixed = mixed + lax.dot_general(rows, low, TN, preferred_element_type=F32)
    out_ref[...] = mixed.astype(BF16)


def combine(rows, pick, weight):
    total, width = rows.shape
    count = pick.shape[1]
    return pl.pallas_call(
        combine_kernel,
        out_shape=jax.ShapeDtypeStruct((width, count), BF16),
        grid=(1,),
        in_specs=[whole(x.shape) for x in (rows, pick, weight)],
        out_specs=whole((width, count)),
        compiler_params=pltpu.CompilerParams(vmem_limit_bytes=VMEM_LIMIT),
        cost_estimate=pl.CostEstimate(flops=4 * total * count * width, bytes_accessed=1500000, transcendentals=0),
    )(rows, pick, weight)


def local(tokens, routes, route_weight, w_gate, w_up, w_down):
    nodes, chips = lax.axis_size("node"), lax.axis_size("y")
    count, width = tokens.shape
    capacity = min(count, 5 * count * routes.shape[1] // (4 * nodes))
    half = capacity // 2
    core, here = lax.axis_index("core").astype(jnp.int32)[None], lax.axis_index("y")
    idx = jnp.concatenate([lax.rem(here + jnp.arange(chips), chips).astype(jnp.int32), core])

    def hop(x, distance):
        return lax.ppermute(x, "y", [(i, (i + distance) % chips) for i in range(chips)])

    def across(x):
        return lax.ppermute(x, "core", SWAP)

    def exchange(x, axes):
        return lax.all_to_all(x, axes, split_axis=0, concat_axis=0, tiled=True)

    own = tokens.T
    rows, pick = dispatch(core, own, across(own), routes.T, nodes, half)
    gate_w, up_w, down_w, rows = lax.optimization_barrier((w_gate[0], w_up[0], w_down[0].T, rows))
    size = nodes * half
    rows = exchange(rows, "node").reshape(size, 2 * width)
    weights = (gate_w, up_w, across(gate_w), across(up_w))

    up_y, down_y = hop(rows, 1), hop(rows, -1)
    sums = gate_up([(0, 0, rows, 0), (0, 0, up_y, chips - 1), (0, 0, down_y, 1)], [], weights, idx)
    for s in range(2, chips // 2):
        up_y, down_y = hop(up_y, 1), hop(down_y, -1)
        new = gate_up([(0, 0, up_y, chips - s), (0, 0, down_y, s)], sums, weights, idx)
        up_y, down_y, down_w, *sums = lax.optimization_barrier((up_y, down_y, down_w, *sums))
        sums = new
    far = chips // 2
    items = [(0, 0, hop(up_y[: size // 2], 1), far), (0, size // 2, hop(down_y[size // 2 :], -1), far)]
    down_other = across(down_w)
    hidden = exchange(gate_up(items, sums, weights, idx, last=(chips, size, 2 * gate_w.shape[1]))[0], "y")
    out = down(core, hidden, down_w, down_other, nodes)
    back = exchange(out.reshape(2 * nodes, half, width), ("node", "core"))
    return combine(back.reshape(2 * nodes * half, width), pick, route_weight.T).T


def solution(mesh):
    shape = mesh.devices.shape
    split = Mesh(mesh.devices.reshape(shape[:2] + (shape[2] // 2, 2)), ("dp", "node", "y", "core"))
    rows, cols = ("dp", "node"), ("y", "core")
    return jax.shard_map(
        local,
        mesh=split,
        in_specs=(
            P(rows, cols),
            P(rows, None),
            P(rows, None),
            P("node", None, cols),
            P("node", None, cols),
            P("node", None, cols),
        ),
        out_specs=P(rows, cols),
        check_vma=False,
    )
```

```python
import functools

import jax
import jax.numpy as jnp
from jax import lax
from jax.experimental import pallas as pl
from jax.experimental.pallas import tpu as pltpu
from jax.sharding import Mesh, PartitionSpec as P

F32, BF16 = jnp.float32, jnp.bfloat16
SWAP = [(0, 1), (1, 0)]
VMEM_LIMIT = 52 * 1024 * 1024
NT = (((1,), (1,)), ((), ()))
TN = (((0,), (0,)), ((), ()))


def whole(shape):
    return pl.BlockSpec(shape, lambda i: (0,) * len(shape))


def dispatch_kernel(core_ref, own_ref, other_ref, routes_ref, rows_ref, pick_ref, both):
    width, count = own_ref.shape
    nodes, half, _ = rows_ref.shape
    core = core_ref[0]
    both[pl.ds(pl.multiple_of(core * width, width), width), :] = own_ref[...]
    both[pl.ds(pl.multiple_of((1 - core) * width, width), width), :] = other_ref[...]
    first, second = routes_ref[0:1, :], routes_ref[1:2, :]
    experts = lax.broadcasted_iota(jnp.int32, (8, count), 0)
    member = (first == experts) | (second == experts)
    before = lax.broadcasted_iota(jnp.int32, (count, count), 0)
    after = lax.broadcasted_iota(jnp.int32, (count, count), 1)
    slots = jnp.dot(
        member.astype(F32).astype(BF16),
        (before < after).astype(F32).astype(BF16),
        preferred_element_type=F32,
    ).astype(jnp.int32)
    for k, route in enumerate((first, second)):
        slot = jnp.sum(jnp.where(route == experts, slots, 0), axis=0, keepdims=True)
        pick_ref[k : k + 1, :] = route * (2 * half) + slot
    wanted = lax.broadcasted_iota(jnp.int32, (half, count), 0) + core * half
    for e in range(nodes):
        chosen = (first == e) | (second == e)
        place = jnp.where(chosen, slots[e : e + 1, :], -1)
        picker = (wanted == place).astype(F32).astype(BF16)
        rows_ref[e] = lax.dot_general(picker, both[...], NT, preferred_element_type=F32).astype(BF16)


def dispatch(core, own, other, routes, nodes, half):
    width, count = own.shape
    return pl.pallas_call(
        dispatch_kernel,
        out_shape=(
            jax.ShapeDtypeStruct((nodes, half, 2 * width), BF16),
            jax.ShapeDtypeStruct((2, count), jnp.int32),
        ),
        grid=(1,),
        in_specs=[pl.BlockSpec(memory_space=pltpu.SMEM)] + [whole(x.shape) for x in (own, other, routes)],
        out_specs=(whole((nodes, half, 2 * width)), whole((2, count))),
        scratch_shapes=[pltpu.VMEM((2 * width, count), BF16)],
        compiler_params=pltpu.CompilerParams(vmem_limit_bytes=VMEM_LIMIT),
        cost_estimate=pl.CostEstimate(flops=2 * nodes * half * count * 2 * width, bytes_accessed=2000000, transcendentals=0),
    )(core, own, other, routes)


def form_hidden(value, core, out, at):
    size, hid = value.shape[0], value.shape[1] // 4
    gate, up = value[:, :hid], value[:, hid : 2 * hid]
    own = gate / (1.0 + jnp.exp(-gate)) * up
    gate, up = value[:, 2 * hid : 3 * hid], value[:, 3 * hid :]
    other = gate / (1.0 + jnp.exp(-gate)) * up
    left = jnp.where(core == 0, own, other).astype(BF16)
    right = jnp.where(core == 0, other, own).astype(BF16)
    for k in range(out.shape[0]):
        out[k, at : at + size, :hid] = left
        out[k, at : at + size, hid:] = right


def join_kernel(*refs):
    hid = refs[0].shape[1]
    for j, ref in enumerate(refs[:-1]):
        refs[-1][:, j * hid : (j + 1) * hid] = ref[...]


def join(parts):
    depth, hid = parts[0].shape
    step = depth // 4
    return pl.pallas_call(
        join_kernel,
        grid=(depth // step,),
        out_shape=jax.ShapeDtypeStruct((depth, len(parts) * hid), BF16),
        in_specs=[pl.BlockSpec((step, hid), lambda k: (k, 0))] * len(parts),
        out_specs=pl.BlockSpec((step, len(parts) * hid), lambda k: (k, 0)),
        compiler_params=pltpu.CompilerParams(vmem_limit_bytes=VMEM_LIMIT),
        cost_estimate=pl.CostEstimate(flops=0, bytes_accessed=4 * depth * hid * len(parts), transcendentals=0),
    )(*parts)


def gate_up_kernel(layout, acc_in, last, idx_ref, *refs):
    count = len(layout)
    blocks, weights = refs[:count], refs[count : 2 * count]
    sums = refs[2 * count : 2 * count + acc_in]
    outs = refs[2 * count + acc_in :]
    total = [s[...] for s in sums] if acc_in else [None] * (1 + max(c for c, _ in layout))
    for j, (chain, at) in enumerate(layout):
        part = jnp.dot(blocks[j][...], weights[j][...], preferred_element_type=F32)
        if total[chain] is None:
            total[chain] = part
        elif part.shape == total[chain].shape:
            total[chain] = total[chain] + part
        else:
            size = part.shape[0]
            pieces = [total[chain][:at], total[chain][at : at + size] + part, total[chain][at + size :]]
            total[chain] = jnp.concatenate([p for p in pieces if p.shape[0]], axis=0)
    if not last:
        for out, value in zip(outs, total):
            out[...] = value
        return
    at = 0
    for value in total:
        form_hidden(value, idx_ref[idx_ref.shape[0] - 1], outs[0], at)
        at += value.shape[0]


def gate_up(items, sums, weights, idx, last=None):
    layout = tuple((c, at) for c, at, _, _ in items)
    blocks = [b for _, _, b, _ in items]
    width, hid = blocks[0].shape[1], weights.shape[1] // 4
    full = lambda shape: pl.BlockSpec(shape, lambda i, idx: (0,) * len(shape))
    in_specs = [full(b.shape) for b in blocks]
    operands = list(blocks)
    for j in range(len(items)):
        in_specs.append(pl.BlockSpec((width, 4 * hid), functools.partial(lambda at, i, idx: (idx[at], 0), items[j][3])))
        operands.append(weights)
    first_sum = 1 + len(operands)
    for s in sums:
        in_specs.append(full(s.shape))
        operands.append(s)
    if last is not None:
        shapes = [jax.ShapeDtypeStruct(last, BF16)]
        aliases = {}
    elif sums:
        shapes = [jax.ShapeDtypeStruct(s.shape, F32) for s in sums]
        aliases = {first_sum + k: k for k in range(len(sums))}
    else:
        sizes = {}
        for c, _, b, _ in items:
            sizes[c] = b.shape[0]
        shapes = [jax.ShapeDtypeStruct((sizes[c], 4 * hid), F32) for c in sorted(sizes)]
        aliases = {}
    rows = sum(b.shape[0] for b in blocks)
    return pl.pallas_call(
        functools.partial(gate_up_kernel, layout, len(sums), last is not None),
        grid_spec=pltpu.PrefetchScalarGridSpec(
            num_scalar_prefetch=1,
            grid=(1,),
            in_specs=in_specs,
            out_specs=[full(s.shape) for s in shapes],
        ),
        out_shape=shapes,
        input_output_aliases=aliases,
        compiler_params=pltpu.CompilerParams(vmem_limit_bytes=VMEM_LIMIT),
        cost_estimate=pl.CostEstimate(
            flops=2 * rows * width * 4 * hid, bytes_accessed=len(items) * 4 * width * hid * 2 + 4 * rows * width, transcendentals=0
        ),
    )(idx, *operands)


def down_kernel(core_ref, hidden_ref, weight_ref, out_ref, total):
    k = pl.program_id(0)
    chips, _, depth = hidden_ref.shape
    part = None
    for j in range(chips):
        term = jnp.dot(hidden_ref[j], weight_ref[j * depth : (j + 1) * depth, :], preferred_element_type=F32)
        part = term if part is None else part + term

    @pl.when(k == 0)
    def _():
        total[...] = part

    @pl.when(k > 0)
    def _():
        total[...] += part

    @pl.when(k == pl.num_programs(0) - 1)
    def _():
        nodes, _, half, width = out_ref.shape
        core = core_ref[0]
        for side, at in ((core, 0), (1 - core, width)):
            for e in range(nodes):
                out_ref[e, side] = total[e * half : (e + 1) * half, at : at + width].astype(BF16)


def down(core, hidden, weights, half):
    chips, rows, depth = hidden.shape
    width = weights.shape[1] // 2
    nodes = rows // half
    step = 2
    return pl.pallas_call(
        down_kernel,
        grid=(chips // step,),
        out_shape=jax.ShapeDtypeStruct((nodes, 2, half, width), BF16),
        in_specs=[
            pl.BlockSpec(memory_space=pltpu.SMEM),
            pl.BlockSpec((step, rows, depth), lambda k: (k, 0, 0)),
            pl.BlockSpec((step * depth, 2 * width), lambda k: (k, 0)),
        ],
        out_specs=pl.BlockSpec((nodes, 2, half, width), lambda k: (0, 0, 0, 0)),
        scratch_shapes=[pltpu.VMEM((rows, 2 * width), F32)],
        compiler_params=pltpu.CompilerParams(vmem_limit_bytes=VMEM_LIMIT),
        cost_estimate=pl.CostEstimate(flops=4 * rows * depth * chips * width, bytes_accessed=6000000, transcendentals=0),
    )(core, hidden, weights)


def combine_kernel(rows_ref, pick_ref, weight_ref, out_ref):
    total = rows_ref.shape[0]
    count = pick_ref.shape[1]
    row = lax.broadcasted_iota(jnp.int32, (total, count), 0)
    scale = jnp.zeros((total, count), F32)
    for k in range(pick_ref.shape[0]):
        scale = jnp.where(row == pick_ref[k : k + 1, :], weight_ref[k : k + 1, :], scale)
    high = scale.astype(BF16)
    low = (scale - high.astype(F32)).astype(BF16)
    rows = rows_ref[...]
    mixed = lax.dot_general(rows, high, TN, preferred_element_type=F32)
    mixed = mixed + lax.dot_general(rows, low, TN, preferred_element_type=F32)
    out_ref[...] = mixed.astype(BF16)


def combine(rows, pick, weight):
    total, width = rows.shape
    count = pick.shape[1]
    return pl.pallas_call(
        combine_kernel,
        out_shape=jax.ShapeDtypeStruct((width, count), BF16),
        grid=(1,),
        in_specs=[whole(x.shape) for x in (rows, pick, weight)],
        out_specs=whole((width, count)),
        compiler_params=pltpu.CompilerParams(vmem_limit_bytes=VMEM_LIMIT),
        cost_estimate=pl.CostEstimate(flops=4 * total * count * width, bytes_accessed=1500000, transcendentals=0),
    )(rows, pick, weight)


def local(tokens, routes, route_weight, w_gate, w_up, w_down):
    nodes, chips = lax.axis_size("node"), lax.axis_size("y")
    count, width = tokens.shape
    capacity = min(count, 5 * count * routes.shape[1] // (4 * nodes))
    half = capacity // 2
    core, here = lax.axis_index("core").astype(jnp.int32)[None], lax.axis_index("y")
    idx = jnp.concatenate([lax.rem(here + jnp.arange(chips), chips).astype(jnp.int32), core])

    def hop(x, distance):
        return lax.ppermute(x, "y", [(i, (i + distance) % chips) for i in range(chips)])

    def across(x):
        return lax.ppermute(x, "core", SWAP)

    def exchange(x, axes):
        return lax.all_to_all(x, axes, split_axis=0, concat_axis=0, tiled=True)

    own = tokens.T
    rows, pick = dispatch(core, own, across(own), routes.T, nodes, half)
    size = nodes * half
    gate_w, up_w, rows = lax.optimization_barrier((w_gate[0], w_up[0], rows))
    rows = exchange(rows, "node").reshape(size, 2 * width)
    weights = join([gate_w, up_w, across(gate_w), across(up_w)])

    up_1, down_1 = hop(rows, 1), hop(rows, -1)
    up_2, down_2 = hop(up_1, 1), hop(down_1, -1)
    sums = gate_up([(0, 0, rows, 0), (0, 0, up_1, chips - 1), (0, 0, down_1, 1)], [], weights, idx)
    up_2, down_2, down_w, *sums = lax.optimization_barrier((up_2, down_2, w_down[0], *sums))
    up_3, down_3 = hop(up_2, 1), hop(down_2, -1)
    up_4, down_4 = hop(up_2[: size // 2], 2), hop(down_2[size // 2 :], -2)
    sums = gate_up([(0, 0, up_2, chips - 2), (0, 0, down_2, 2)], sums, weights, idx)
    sums = gate_up([(0, 0, up_3, chips - 3), (0, 0, down_3, 3)], sums, weights, idx)
    items = [(0, 0, up_4, 4), (0, size // 2, down_4, 4)]
    hidden = exchange(gate_up(items, sums, weights, idx, (chips, size, weights.shape[1] // 2))[0], "y")
    down_weights = jnp.concatenate([down_w, across(down_w)], axis=1)
    out = down(core, hidden, down_weights, half)
    back = exchange(out.reshape(2 * nodes, half, width), ("node", "core"))
    return combine(back.reshape(2 * nodes * half, width), pick, route_weight.T).T


def solution(mesh):
    shape = mesh.devices.shape
    split = Mesh(mesh.devices.reshape(shape[:2] + (shape[2] // 2, 2)), ("dp", "node", "y", "core"))
    rows, cols = ("dp", "node"), ("y", "core")
    return jax.shard_map(
        local,
        mesh=split,
        in_specs=(
            P(rows, cols),
            P(rows, None),
            P(rows, None),
            P("node", None, cols),
            P("node", None, cols),
            P("node", None, cols),
        ),
        out_specs=P(rows, cols),
        check_vma=False,
    )
```

```python
import functools

import jax
import jax.numpy as jnp
from jax import lax
from jax.experimental import pallas as pl
from jax.experimental.pallas import tpu as pltpu
from jax.sharding import Mesh, PartitionSpec as P

F32, BF16 = jnp.float32, jnp.bfloat16
SWAP = [(0, 1), (1, 0)]
VMEM_LIMIT = 52 * 1024 * 1024
NT = (((1,), (1,)), ((), ()))
TN = (((0,), (0,)), ((), ()))


def whole(shape):
    return pl.BlockSpec(shape, lambda i: (0,) * len(shape))


def dispatch_kernel(core_ref, own_ref, other_ref, routes_ref, rows_ref, pick_ref, both):
    width, count = own_ref.shape
    nodes, half, _ = rows_ref.shape
    core = core_ref[0]
    both[pl.ds(pl.multiple_of(core * width, width), width), :] = own_ref[...]
    both[pl.ds(pl.multiple_of((1 - core) * width, width), width), :] = other_ref[...]
    first, second = routes_ref[0:1, :], routes_ref[1:2, :]
    experts = lax.broadcasted_iota(jnp.int32, (8, count), 0)
    member = (first == experts) | (second == experts)
    before = lax.broadcasted_iota(jnp.int32, (count, count), 0)
    after = lax.broadcasted_iota(jnp.int32, (count, count), 1)
    slots = jnp.dot(
        member.astype(F32).astype(BF16),
        (before < after).astype(F32).astype(BF16),
        preferred_element_type=F32,
    ).astype(jnp.int32)
    for k, route in enumerate((first, second)):
        slot = jnp.sum(jnp.where(route == experts, slots, 0), axis=0, keepdims=True)
        pick_ref[k : k + 1, :] = route * (2 * half) + slot
    wanted = lax.broadcasted_iota(jnp.int32, (half, count), 0) + core * half
    for e in range(nodes):
        chosen = (first == e) | (second == e)
        place = jnp.where(chosen, slots[e : e + 1, :], -1)
        picker = (wanted == place).astype(F32).astype(BF16)
        rows_ref[e] = lax.dot_general(picker, both[...], NT, preferred_element_type=F32).astype(BF16)


def dispatch(core, own, other, routes, nodes, half):
    width, count = own.shape
    return pl.pallas_call(
        dispatch_kernel,
        out_shape=(
            jax.ShapeDtypeStruct((nodes, half, 2 * width), BF16),
            jax.ShapeDtypeStruct((2, count), jnp.int32),
        ),
        grid=(1,),
        in_specs=[pl.BlockSpec(memory_space=pltpu.SMEM)] + [whole(x.shape) for x in (own, other, routes)],
        out_specs=(whole((nodes, half, 2 * width)), whole((2, count))),
        scratch_shapes=[pltpu.VMEM((2 * width, count), BF16)],
        compiler_params=pltpu.CompilerParams(vmem_limit_bytes=VMEM_LIMIT),
        cost_estimate=pl.CostEstimate(flops=2 * nodes * half * count * 2 * width, bytes_accessed=2000000, transcendentals=0),
    )(core, own, other, routes)


def gate_up_kernel(layout, rest, last, idx_ref, *refs):
    refs = list(refs)
    x = []
    for parts in layout:
        x.append(jnp.concatenate([refs.pop(0)[...] for _ in range(parts)], axis=0))
    w = []
    for _ in layout:
        w.append(jnp.concatenate([refs.pop(0)[...] for _ in range(4)], axis=1))
    total = jnp.dot(jnp.concatenate(x, axis=1), jnp.concatenate(w, axis=0), preferred_element_type=F32)
    if rest:
        total = total + refs.pop(0)[...]
    out = refs.pop(0)
    if not last:
        out[...] = total
        return
    core = idx_ref[idx_ref.shape[0] - 1]
    hid = total.shape[1] // 4
    gate, up = total[:, :hid], total[:, hid : 2 * hid]
    own = gate / (1.0 + jnp.exp(-gate)) * up
    gate, up = total[:, 2 * hid : 3 * hid], total[:, 3 * hid :]
    other = gate / (1.0 + jnp.exp(-gate)) * up
    left = jnp.where(core == 0, own, other).astype(BF16)
    right = jnp.where(core == 0, other, own).astype(BF16)
    for k in range(out.shape[0]):
        out[k, :, :hid] = left
        out[k, :, hid:] = right


def gate_up(items, sums, weights, idx, last=None):
    operands = [b for blocks, _ in items for b in blocks]
    rows = sum(b.shape[0] for b in items[0][0])
    width, hid = operands[0].shape[1], weights[0].shape[1]
    full = lambda shape: pl.BlockSpec(shape, lambda i, idx: (0,) * len(shape))
    in_specs = [full(b.shape) for b in operands]
    for _, at in items:
        for w in weights:
            in_specs.append(pl.BlockSpec((width, hid), functools.partial(lambda at, i, idx: (idx[at], 0), at)))
            operands.append(w)
    aliases = {}
    if sums is not None:
        if last is None:
            aliases[1 + len(operands)] = 0
        in_specs.append(full(sums.shape))
        operands.append(sums)
    shape = jax.ShapeDtypeStruct((rows, 4 * hid), F32)
    if last is not None:
        shape = jax.ShapeDtypeStruct((last, rows, 2 * hid), BF16)
    return pl.pallas_call(
        functools.partial(
            gate_up_kernel, tuple(len(blocks) for blocks, _ in items), sums is not None, last is not None
        ),
        grid_spec=pltpu.PrefetchScalarGridSpec(
            num_scalar_prefetch=1, grid=(1,), in_specs=in_specs, out_specs=full(shape.shape)
        ),
        out_shape=shape,
        input_output_aliases=aliases,
        compiler_params=pltpu.CompilerParams(vmem_limit_bytes=VMEM_LIMIT),
        cost_estimate=pl.CostEstimate(
            flops=8 * len(items) * rows * width * hid,
            bytes_accessed=len(items) * width * (8 * hid + 2 * rows) + 16 * rows * hid,
            transcendentals=0,
        ),
    )(idx, *operands)


def down_kernel(core_ref, hidden_ref, own_ref, other_ref, out_ref, total):
    k = pl.program_id(0)
    hidden = jnp.concatenate([hidden_ref[j] for j in range(hidden_ref.shape[0])], axis=1)
    w = jnp.concatenate([own_ref[...], other_ref[...]], axis=0)
    part = lax.dot_general(hidden, w, NT, preferred_element_type=F32)

    @pl.when(k == 0)
    def _():
        total[...] = part

    @pl.when(k > 0)
    def _():
        nodes, _, half, width = out_ref.shape
        core = core_ref[0]
        for side, at in ((core, 0), (1 - core, width)):
            for e in range(nodes):
                rows, cols = slice(e * half, (e + 1) * half), slice(at, at + width)
                out_ref[e, side] = (total[rows, cols] + part[rows, cols]).astype(BF16)


def down(core, hidden, own, other, half):
    chips, rows, depth = hidden.shape
    width = own.shape[0]
    nodes = rows // half
    step = chips // 2
    return pl.pallas_call(
        down_kernel,
        grid=(2,),
        out_shape=jax.ShapeDtypeStruct((nodes, 2, half, width), BF16),
        in_specs=[
            pl.BlockSpec(memory_space=pltpu.SMEM),
            pl.BlockSpec((step, rows, depth), lambda k: (k, 0, 0)),
            pl.BlockSpec((width, step * depth), lambda k: (0, k)),
            pl.BlockSpec((width, step * depth), lambda k: (0, k)),
        ],
        out_specs=pl.BlockSpec((nodes, 2, half, width), lambda k: (0, 0, 0, 0)),
        scratch_shapes=[pltpu.VMEM((rows, 2 * width), F32)],
        compiler_params=pltpu.CompilerParams(vmem_limit_bytes=VMEM_LIMIT),
        cost_estimate=pl.CostEstimate(flops=4 * rows * depth * chips * width, bytes_accessed=6000000, transcendentals=0),
    )(core, hidden, own, other)


def combine_kernel(rows_ref, pick_ref, weight_ref, out_ref):
    total = rows_ref.shape[0]
    count = pick_ref.shape[1]
    row = lax.broadcasted_iota(jnp.int32, (total, count), 0)
    scale = jnp.zeros((total, count), F32)
    for k in range(pick_ref.shape[0]):
        scale = jnp.where(row == pick_ref[k : k + 1, :], weight_ref[k : k + 1, :], scale)
    high = scale.astype(BF16)
    low = (scale - high.astype(F32)).astype(BF16)
    rows = rows_ref[...]
    mixed = lax.dot_general(rows, high, TN, preferred_element_type=F32)
    mixed = mixed + lax.dot_general(rows, low, TN, preferred_element_type=F32)
    out_ref[...] = mixed.astype(BF16)


def combine(rows, pick, weight):
    total, width = rows.shape
    count = pick.shape[1]
    return pl.pallas_call(
        combine_kernel,
        out_shape=jax.ShapeDtypeStruct((width, count), BF16),
        grid=(1,),
        in_specs=[whole(x.shape) for x in (rows, pick, weight)],
        out_specs=whole((width, count)),
        compiler_params=pltpu.CompilerParams(vmem_limit_bytes=VMEM_LIMIT),
        cost_estimate=pl.CostEstimate(flops=4 * total * count * width, bytes_accessed=1500000, transcendentals=0),
    )(rows, pick, weight)


def local(tokens, routes, route_weight, w_gate, w_up, w_down):
    nodes, chips = lax.axis_size("node"), lax.axis_size("y")
    count, width = tokens.shape
    capacity = min(count, 5 * count * routes.shape[1] // (4 * nodes))
    half = capacity // 2
    core, here = lax.axis_index("core").astype(jnp.int32)[None], lax.axis_index("y")
    idx = jnp.concatenate([lax.rem(here + jnp.arange(chips), chips).astype(jnp.int32), core])

    def hop(x, distance):
        return lax.ppermute(x, "y", [(i, (i + distance) % chips) for i in range(chips)])

    def across(x):
        return lax.ppermute(x, "core", SWAP)

    def exchange(x, axes):
        return lax.all_to_all(x, axes, split_axis=0, concat_axis=0, tiled=True)

    own = tokens.T
    rows, pick = dispatch(core, own, across(own), routes.T, nodes, half)
    size = nodes * half
    gate_w, up_w, rows = lax.optimization_barrier((w_gate[0], w_up[0], rows))
    rows = exchange(rows, "node").reshape(size, 2 * width)
    weights = (gate_w, up_w, across(gate_w), across(up_w))

    up_1, down_1 = hop(rows, 1), hop(rows, -1)
    up_2, down_2 = hop(up_1, 1), hop(down_1, -1)
    sums = gate_up([((rows,), 0), ((up_1,), chips - 1), ((down_1,), 1)], None, weights, idx)
    up_2, down_2, down_w, sums = lax.optimization_barrier((up_2, down_2, w_down[0].T, sums))
    up_3, down_3 = hop(up_2, 1), hop(down_2, -1)
    up_4, down_4 = hop(up_2[: size // 2], 2), hop(down_2[size // 2 :], -2)
    sums = gate_up([((up_2,), chips - 2), ((down_2,), 2)], sums, weights, idx)
    sums, down_other = lax.optimization_barrier((sums, across(down_w)))
    sums = gate_up([((up_3,), chips - 3), ((down_3,), 3)], sums, weights, idx)
    hidden = exchange(gate_up([((up_4, down_4), 4)], sums, weights, idx, last=chips), "y")
    out = down(core, hidden, down_w, down_other, half)
    back = exchange(out.reshape(2 * nodes, half, width), ("node", "core"))
    return combine(back.reshape(2 * nodes * half, width), pick, route_weight.T).T


def solution(mesh):
    shape = mesh.devices.shape
    split = Mesh(mesh.devices.reshape(shape[:2] + (shape[2] // 2, 2)), ("dp", "node", "y", "core"))
    rows, cols = ("dp", "node"), ("y", "core")
    return jax.shard_map(
        local,
        mesh=split,
        in_specs=(
            P(rows, cols),
            P(rows, None),
            P(rows, None),
            P("node", None, cols),
            P("node", None, cols),
            P("node", None, cols),
        ),
        out_specs=P(rows, cols),
        check_vma=False,
    )
```

```python
import functools

import jax
import jax.numpy as jnp
from jax import lax
from jax.experimental import pallas as pl
from jax.experimental.pallas import tpu as pltpu
from jax.sharding import Mesh, PartitionSpec as P

F32, BF16 = jnp.float32, jnp.bfloat16
SWAP = [(0, 1), (1, 0)]
VMEM_LIMIT = 52 * 1024 * 1024
LAST_LIMIT = 32 * 1024 * 1024
NT = (((1,), (1,)), ((), ()))
TN = (((0,), (0,)), ((), ()))


def whole(shape):
    return pl.BlockSpec(shape, lambda i: (0,) * len(shape))


def dispatch_kernel(core_ref, own_ref, other_ref, routes_ref, rows_ref, pick_ref, both):
    width, count = own_ref.shape
    nodes, half, _ = rows_ref.shape
    core = core_ref[0]
    both[pl.ds(pl.multiple_of(core * width, width), width), :] = own_ref[...]
    both[pl.ds(pl.multiple_of((1 - core) * width, width), width), :] = other_ref[...]
    first, second = routes_ref[0:1, :], routes_ref[1:2, :]
    experts = lax.broadcasted_iota(jnp.int32, (8, count), 0)
    member = (first == experts) | (second == experts)
    before = lax.broadcasted_iota(jnp.int32, (count, count), 0)
    after = lax.broadcasted_iota(jnp.int32, (count, count), 1)
    slots = jnp.dot(
        member.astype(F32).astype(BF16),
        (before < after).astype(F32).astype(BF16),
        preferred_element_type=F32,
    ).astype(jnp.int32)
    for k, route in enumerate((first, second)):
        slot = jnp.sum(jnp.where(route == experts, slots, 0), axis=0, keepdims=True)
        pick_ref[k : k + 1, :] = route * (2 * half) + slot
    wanted = lax.broadcasted_iota(jnp.int32, (half, count), 0) + core * half
    for e in range(nodes):
        chosen = (first == e) | (second == e)
        place = jnp.where(chosen, slots[e : e + 1, :], -1)
        picker = (wanted == place).astype(F32).astype(BF16)
        rows_ref[e] = lax.dot_general(picker, both[...], NT, preferred_element_type=F32).astype(BF16)


def dispatch(core, own, other, routes, nodes, half):
    width, count = own.shape
    return pl.pallas_call(
        dispatch_kernel,
        out_shape=(
            jax.ShapeDtypeStruct((nodes, half, 2 * width), BF16),
            jax.ShapeDtypeStruct((2, count), jnp.int32),
        ),
        grid=(1,),
        in_specs=[pl.BlockSpec(memory_space=pltpu.SMEM)] + [whole(x.shape) for x in (own, other, routes)],
        out_specs=(whole((nodes, half, 2 * width)), whole((2, count))),
        scratch_shapes=[pltpu.VMEM((2 * width, count), BF16)],
        compiler_params=pltpu.CompilerParams(vmem_limit_bytes=VMEM_LIMIT),
        cost_estimate=pl.CostEstimate(flops=2 * nodes * half * count * 2 * width, bytes_accessed=2000000, transcendentals=0),
    )(core, own, other, routes)


def gate_up_kernel(layout, rest, last, idx_ref, *refs):
    refs = list(refs)
    x = []
    for parts in layout:
        x.append(jnp.concatenate([refs.pop(0)[...] for _ in range(parts)], axis=0))
    w = []
    for _ in layout:
        w.append(jnp.concatenate([refs.pop(0)[...] for _ in range(4)], axis=1))
    total = jnp.dot(jnp.concatenate(x, axis=1), jnp.concatenate(w, axis=0), preferred_element_type=F32)
    if rest:
        total = total + refs.pop(0)[...]
    out = refs.pop(0)
    if not last:
        out[...] = total
        return
    core = idx_ref[idx_ref.shape[0] - 1]
    hid = total.shape[1] // 4
    gate, up = total[:, :hid], total[:, hid : 2 * hid]
    own = gate / (1.0 + jnp.exp(-gate)) * up
    gate, up = total[:, 2 * hid : 3 * hid], total[:, 3 * hid :]
    other = gate / (1.0 + jnp.exp(-gate)) * up
    left = jnp.where(core == 0, own, other).astype(BF16)
    right = jnp.where(core == 0, other, own).astype(BF16)
    for k in range(out.shape[0]):
        out[k, :, :hid] = left
        out[k, :, hid:] = right


def gate_up(items, sums, weights, idx, last=None):
    operands = [b for blocks, _ in items for b in blocks]
    rows = sum(b.shape[0] for b in items[0][0])
    width, hid = operands[0].shape[1], weights[0].shape[1]
    full = lambda shape: pl.BlockSpec(shape, lambda i, idx: (0,) * len(shape))
    in_specs = [full(b.shape) for b in operands]
    for _, at in items:
        for w in weights:
            in_specs.append(pl.BlockSpec((width, hid), functools.partial(lambda at, i, idx: (idx[at], 0), at)))
            operands.append(w)
    aliases = {}
    if sums is not None:
        if last is None:
            aliases[1 + len(operands)] = 0
        in_specs.append(full(sums.shape))
        operands.append(sums)
    shape = jax.ShapeDtypeStruct((rows, 4 * hid), F32)
    if last is not None:
        shape = jax.ShapeDtypeStruct((last, rows, 2 * hid), BF16)
    return pl.pallas_call(
        functools.partial(
            gate_up_kernel, tuple(len(blocks) for blocks, _ in items), sums is not None, last is not None
        ),
        grid_spec=pltpu.PrefetchScalarGridSpec(
            num_scalar_prefetch=1, grid=(1,), in_specs=in_specs, out_specs=full(shape.shape)
        ),
        out_shape=shape,
        input_output_aliases=aliases,
        compiler_params=pltpu.CompilerParams(vmem_limit_bytes=VMEM_LIMIT if last is None else LAST_LIMIT),
        cost_estimate=pl.CostEstimate(
            flops=8 * len(items) * rows * width * hid,
            bytes_accessed=len(items) * width * (8 * hid + 2 * rows) + 16 * rows * hid,
            transcendentals=0,
        ),
    )(idx, *operands)


def down_kernel(core_ref, hidden_ref, own_ref, other_ref, out_ref, total):
    k = pl.program_id(0)
    hidden = jnp.concatenate([hidden_ref[j] for j in range(hidden_ref.shape[0])], axis=1)
    w = jnp.concatenate([own_ref[...], other_ref[...]], axis=0)
    part = lax.dot_general(hidden, w, NT, preferred_element_type=F32)

    @pl.when(k == 0)
    def _():
        total[...] = part

    @pl.when(k > 0)
    def _():
        nodes, _, half, width = out_ref.shape
        core = core_ref[0]
        for side, at in ((core, 0), (1 - core, width)):
            for e in range(nodes):
                rows, cols = slice(e * half, (e + 1) * half), slice(at, at + width)
                out_ref[e, side] = (total[rows, cols] + part[rows, cols]).astype(BF16)


def down(core, hidden, own, other, half):
    chips, rows, depth = hidden.shape
    width = own.shape[0]
    nodes = rows // half
    step = chips // 2
    return pl.pallas_call(
        down_kernel,
        grid=(2,),
        out_shape=jax.ShapeDtypeStruct((nodes, 2, half, width), BF16),
        in_specs=[
            pl.BlockSpec(memory_space=pltpu.SMEM),
            pl.BlockSpec((step, rows, depth), lambda k: (k, 0, 0)),
            pl.BlockSpec((width, step * depth), lambda k: (0, k)),
            pl.BlockSpec((width, step * depth), lambda k: (0, k)),
        ],
        out_specs=pl.BlockSpec((nodes, 2, half, width), lambda k: (0, 0, 0, 0)),
        scratch_shapes=[pltpu.VMEM((rows, 2 * width), F32)],
        compiler_params=pltpu.CompilerParams(vmem_limit_bytes=VMEM_LIMIT),
        cost_estimate=pl.CostEstimate(flops=4 * rows * depth * chips * width, bytes_accessed=6000000, transcendentals=0),
    )(core, hidden, own, other)


def combine_kernel(rows_ref, pick_ref, weight_ref, out_ref):
    total = rows_ref.shape[0]
    count = pick_ref.shape[1]
    row = lax.broadcasted_iota(jnp.int32, (total, count), 0)
    scale = jnp.zeros((total, count), F32)
    for k in range(pick_ref.shape[0]):
        scale = jnp.where(row == pick_ref[k : k + 1, :], weight_ref[k : k + 1, :], scale)
    high = scale.astype(BF16)
    low = (scale - high.astype(F32)).astype(BF16)
    rows = rows_ref[...]
    mixed = lax.dot_general(rows, high, TN, preferred_element_type=F32)
    mixed = mixed + lax.dot_general(rows, low, TN, preferred_element_type=F32)
    out_ref[...] = mixed.astype(BF16)


def combine(rows, pick, weight):
    total, width = rows.shape
    count = pick.shape[1]
    return pl.pallas_call(
        combine_kernel,
        out_shape=jax.ShapeDtypeStruct((width, count), BF16),
        grid=(1,),
        in_specs=[whole(x.shape) for x in (rows, pick, weight)],
        out_specs=whole((width, count)),
        compiler_params=pltpu.CompilerParams(vmem_limit_bytes=VMEM_LIMIT),
        cost_estimate=pl.CostEstimate(flops=4 * total * count * width, bytes_accessed=1500000, transcendentals=0),
    )(rows, pick, weight)


def local(tokens, routes, route_weight, w_gate, w_up, w_down):
    nodes, chips = lax.axis_size("node"), lax.axis_size("y")
    count, width = tokens.shape
    capacity = min(count, 5 * count * routes.shape[1] // (4 * nodes))
    half = capacity // 2
    core, here = lax.axis_index("core").astype(jnp.int32)[None], lax.axis_index("y")
    idx = jnp.concatenate([lax.rem(here + jnp.arange(chips), chips).astype(jnp.int32), core])

    def hop(x, distance):
        return lax.ppermute(x, "y", [(i, (i + distance) % chips) for i in range(chips)])

    def across(x):
        return lax.ppermute(x, "core", SWAP)

    def exchange(x, axes):
        return lax.all_to_all(x, axes, split_axis=0, concat_axis=0, tiled=True)

    own = tokens.T
    rows, pick = dispatch(core, own, across(own), routes.T, nodes, half)
    size = nodes * half
    gate_w, up_w, rows = lax.optimization_barrier((w_gate[0], w_up[0], rows))
    rows = exchange(rows, "node").reshape(size, 2 * width)
    weights = (gate_w, up_w, across(gate_w), across(up_w))

    up_1, down_1 = hop(rows, 1), hop(rows, -1)
    up_2, down_2 = hop(up_1, 1), hop(down_1, -1)
    sums = gate_up([((rows,), 0), ((up_1,), chips - 1), ((down_1,), 1)], None, weights, idx)
    up_2, down_2, down_w, sums = lax.optimization_barrier((up_2, down_2, w_down[0].T, sums))
    up_3, down_3 = hop(up_2, 1), hop(down_2, -1)
    up_4, down_4 = hop(up_2[: size // 2], 2), hop(down_2[size // 2 :], -2)
    sums = gate_up([((up_2,), chips - 2), ((down_2,), 2)], sums, weights, idx)
    sums, down_other = lax.optimization_barrier((sums, across(down_w)))
    sums = gate_up([((up_3,), chips - 3), ((down_3,), 3)], sums, weights, idx)
    hidden = exchange(gate_up([((up_4, down_4), 4)], sums, weights, idx, last=chips), "y")
    out = down(core, hidden, down_w, down_other, half)
    back = exchange(out.reshape(2 * nodes, half, width), ("node", "core"))
    return combine(back.reshape(2 * nodes * half, width), pick, route_weight.T).T


def solution(mesh):
    shape = mesh.devices.shape
    split = Mesh(mesh.devices.reshape(shape[:2] + (shape[2] // 2, 2)), ("dp", "node", "y", "core"))
    rows, cols = ("dp", "node"), ("y", "core")
    return jax.shard_map(
        local,
        mesh=split,
        in_specs=(
            P(rows, cols),
            P(rows, None),
            P(rows, None),
            P("node", None, cols),
            P("node", None, cols),
            P("node", None, cols),
        ),
        out_specs=P(rows, cols),
        check_vma=False,
    )
```

```python
import functools

import jax
import jax.numpy as jnp
from jax import lax
from jax.experimental import pallas as pl
from jax.experimental.pallas import tpu as pltpu
from jax.sharding import Mesh, PartitionSpec as P

F32, BF16 = jnp.float32, jnp.bfloat16
SWAP = [(0, 1), (1, 0)]
VMEM_LIMIT = 52 * 1024 * 1024
LAST_LIMIT = 32 * 1024 * 1024
NT = (((1,), (1,)), ((), ()))
TN = (((0,), (0,)), ((), ()))


def whole(shape):
    return pl.BlockSpec(shape, lambda i: (0,) * len(shape))


def dispatch_kernel(core_ref, own_ref, other_ref, routes_ref, rows_ref, pick_ref, both):
    width, count = own_ref.shape
    nodes, half, _ = rows_ref.shape
    core = core_ref[0]
    both[pl.ds(pl.multiple_of(core * width, width), width), :] = own_ref[...]
    both[pl.ds(pl.multiple_of((1 - core) * width, width), width), :] = other_ref[...]
    first, second = routes_ref[0:1, :], routes_ref[1:2, :]
    experts = lax.broadcasted_iota(jnp.int32, (8, count), 0)
    member = (first == experts) | (second == experts)
    before = lax.broadcasted_iota(jnp.int32, (count, count), 0)
    after = lax.broadcasted_iota(jnp.int32, (count, count), 1)
    slots = jnp.dot(
        member.astype(F32).astype(BF16),
        (before < after).astype(F32).astype(BF16),
        preferred_element_type=F32,
    ).astype(jnp.int32)
    for k, route in enumerate((first, second)):
        slot = jnp.sum(jnp.where(route == experts, slots, 0), axis=0, keepdims=True)
        pick_ref[k : k + 1, :] = route * (2 * half) + slot
    wanted = lax.broadcasted_iota(jnp.int32, (half, count), 0) + core * half
    for e in range(nodes):
        chosen = (first == e) | (second == e)
        place = jnp.where(chosen, slots[e : e + 1, :], -1)
        picker = (wanted == place).astype(F32).astype(BF16)
        rows_ref[e] = lax.dot_general(picker, both[...], NT, preferred_element_type=F32).astype(BF16)


def dispatch(core, own, other, routes, nodes, half):
    width, count = own.shape
    return pl.pallas_call(
        dispatch_kernel,
        out_shape=(
            jax.ShapeDtypeStruct((nodes, half, 2 * width), BF16),
            jax.ShapeDtypeStruct((2, count), jnp.int32),
        ),
        grid=(1,),
        in_specs=[pl.BlockSpec(memory_space=pltpu.SMEM)] + [whole(x.shape) for x in (own, other, routes)],
        out_specs=(whole((nodes, half, 2 * width)), whole((2, count))),
        scratch_shapes=[pltpu.VMEM((2 * width, count), BF16)],
        compiler_params=pltpu.CompilerParams(vmem_limit_bytes=VMEM_LIMIT),
        cost_estimate=pl.CostEstimate(flops=2 * nodes * half * count * 2 * width, bytes_accessed=2000000, transcendentals=0),
    )(core, own, other, routes)


def gate_up_kernel(layout, rest, last, idx_ref, *refs):
    refs = list(refs)
    x = []
    for parts in layout:
        x.append(jnp.concatenate([refs.pop(0)[...] for _ in range(parts)], axis=0))
    w = []
    for _ in layout:
        w.append(jnp.concatenate([refs.pop(0)[...] for _ in range(4)], axis=1))
    total = jnp.dot(jnp.concatenate(x, axis=1), jnp.concatenate(w, axis=0), preferred_element_type=F32)
    if rest:
        total = total + refs.pop(0)[...]
    out = refs.pop(0)
    if not last:
        out[...] = total
        return
    core = idx_ref[idx_ref.shape[0] - 1]
    hid = total.shape[1] // 4
    gate, up = total[:, :hid], total[:, hid : 2 * hid]
    own = gate / (1.0 + jnp.exp(-gate)) * up
    gate, up = total[:, 2 * hid : 3 * hid], total[:, 3 * hid :]
    other = gate / (1.0 + jnp.exp(-gate)) * up
    left = jnp.where(core == 0, own, other).astype(BF16)
    right = jnp.where(core == 0, other, own).astype(BF16)
    for k in range(out.shape[0]):
        out[k, :, :hid] = left
        out[k, :, hid:] = right


def gate_up(items, sums, weights, idx, last=None):
    operands = [b for blocks, _ in items for b in blocks]
    rows = sum(b.shape[0] for b in items[0][0])
    width, hid = operands[0].shape[1], weights[0].shape[1]
    full = lambda shape: pl.BlockSpec(shape, lambda i, idx: (0,) * len(shape))
    in_specs = [full(b.shape) for b in operands]
    for _, at in items:
        for w in weights:
            in_specs.append(pl.BlockSpec((width, hid), functools.partial(lambda at, i, idx: (idx[at], 0), at)))
            operands.append(w)
    aliases = {}
    if sums is not None:
        if last is None:
            aliases[1 + len(operands)] = 0
        in_specs.append(full(sums.shape))
        operands.append(sums)
    shape = jax.ShapeDtypeStruct((rows, 4 * hid), F32)
    if last is not None:
        shape = jax.ShapeDtypeStruct((last, rows, 2 * hid), BF16)
    return pl.pallas_call(
        functools.partial(
            gate_up_kernel, tuple(len(blocks) for blocks, _ in items), sums is not None, last is not None
        ),
        grid_spec=pltpu.PrefetchScalarGridSpec(
            num_scalar_prefetch=1, grid=(1,), in_specs=in_specs, out_specs=full(shape.shape)
        ),
        out_shape=shape,
        input_output_aliases=aliases,
        compiler_params=pltpu.CompilerParams(vmem_limit_bytes=VMEM_LIMIT if last is None else LAST_LIMIT),
        cost_estimate=pl.CostEstimate(
            flops=8 * len(items) * rows * width * hid,
            bytes_accessed=len(items) * width * (8 * hid + 2 * rows) + 16 * rows * hid,
            transcendentals=0,
        ),
    )(idx, *operands)


def down_kernel(core_ref, hidden_ref, own_ref, other_ref, out_ref, total):
    k = pl.program_id(0)
    hidden = jnp.concatenate([hidden_ref[j] for j in range(hidden_ref.shape[0])], axis=1)
    w = jnp.concatenate([own_ref[...], other_ref[...]], axis=0)
    part = lax.dot_general(hidden, w, NT, preferred_element_type=F32)

    @pl.when(k == 0)
    def _():
        total[...] = part

    @pl.when(k > 0)
    def _():
        nodes, _, half, width = out_ref.shape
        core = core_ref[0]
        for side, at in ((core, 0), (1 - core, width)):
            for e in range(nodes):
                rows, cols = slice(e * half, (e + 1) * half), slice(at, at + width)
                out_ref[e, side] = (total[rows, cols] + part[rows, cols]).astype(BF16)


def down(core, hidden, own, other, half):
    chips, rows, depth = hidden.shape
    width = own.shape[0]
    nodes = rows // half
    step = chips // 2
    return pl.pallas_call(
        down_kernel,
        grid=(2,),
        out_shape=jax.ShapeDtypeStruct((nodes, 2, half, width), BF16),
        in_specs=[
            pl.BlockSpec(memory_space=pltpu.SMEM),
            pl.BlockSpec((step, rows, depth), lambda k: (k, 0, 0)),
            pl.BlockSpec((width, step * depth), lambda k: (0, k)),
            pl.BlockSpec((width, step * depth), lambda k: (0, k)),
        ],
        out_specs=pl.BlockSpec((nodes, 2, half, width), lambda k: (0, 0, 0, 0)),
        scratch_shapes=[pltpu.VMEM((rows, 2 * width), F32)],
        compiler_params=pltpu.CompilerParams(vmem_limit_bytes=VMEM_LIMIT),
        cost_estimate=pl.CostEstimate(flops=4 * rows * depth * chips * width, bytes_accessed=6000000, transcendentals=0),
    )(core, hidden, own, other)


def combine_kernel(rows_ref, pick_ref, weight_ref, out_ref):
    total = rows_ref.shape[0]
    count = pick_ref.shape[1]
    row = lax.broadcasted_iota(jnp.int32, (total, count), 0)
    scale = jnp.zeros((total, count), F32)
    for k in range(pick_ref.shape[0]):
        scale = jnp.where(row == pick_ref[k : k + 1, :], weight_ref[k : k + 1, :], scale)
    high = scale.astype(BF16)
    low = (scale - high.astype(F32)).astype(BF16)
    rows = rows_ref[...]
    mixed = lax.dot_general(rows, high, TN, preferred_element_type=F32)
    mixed = mixed + lax.dot_general(rows, low, TN, preferred_element_type=F32)
    out_ref[...] = mixed.astype(BF16)


def combine(rows, pick, weight):
    total, width = rows.shape
    count = pick.shape[1]
    return pl.pallas_call(
        combine_kernel,
        out_shape=jax.ShapeDtypeStruct((width, count), BF16),
        grid=(1,),
        in_specs=[whole(x.shape) for x in (rows, pick, weight)],
        out_specs=whole((width, count)),
        compiler_params=pltpu.CompilerParams(vmem_limit_bytes=VMEM_LIMIT),
        cost_estimate=pl.CostEstimate(flops=4 * total * count * width, bytes_accessed=1500000, transcendentals=0),
    )(rows, pick, weight)


def local(tokens, routes, route_weight, w_gate, w_up, w_down):
    nodes, chips = lax.axis_size("node"), lax.axis_size("y")
    count, width = tokens.shape
    capacity = min(count, 5 * count * routes.shape[1] // (4 * nodes))
    half = capacity // 2
    core, here = lax.axis_index("core").astype(jnp.int32)[None], lax.axis_index("y")
    idx = jnp.concatenate([lax.rem(here + jnp.arange(chips), chips).astype(jnp.int32), core])

    def hop(x, distance):
        return lax.ppermute(x, "y", [(i, (i + distance) % chips) for i in range(chips)])

    def across(x):
        return lax.ppermute(x, "core", SWAP)

    def exchange(x, axes):
        return lax.all_to_all(x, axes, split_axis=0, concat_axis=0, tiled=True)

    own = tokens.T
    rows, pick = dispatch(core, own, across(own), routes.T, nodes, half)
    size = nodes * half
    gate_w, up_w, rows = lax.optimization_barrier((w_gate[0], w_up[0], rows))
    rows = exchange(rows, "node").reshape(size, 2 * width)
    weights = (gate_w, up_w, across(gate_w), across(up_w))

    up_y, down_y = hop(rows, 1), hop(rows, -1)
    sums = gate_up([((rows,), 0), ((up_y,), chips - 1), ((down_y,), 1)], None, weights, idx)
    for s in range(2, chips // 2):
        up_y, down_y = hop(up_y, 1), hop(down_y, -1)
        new = gate_up([((up_y,), chips - s), ((down_y,), s)], sums, weights, idx)
        up_y, down_y, sums = lax.optimization_barrier((up_y, down_y, sums))
        sums = new
    far = (hop(up_y[: size // 2], 1), hop(down_y[size // 2 :], -1))
    hidden = gate_up([(far, chips // 2)], sums, weights, idx, last=chips)
    hidden, down_w = lax.optimization_barrier((hidden, w_down[0].T))
    hidden, down_other = exchange(hidden, "y"), across(down_w)
    out = down(core, hidden, down_w, down_other, half)
    back = exchange(out.reshape(2 * nodes, half, width), ("node", "core"))
    return combine(back.reshape(2 * nodes * half, width), pick, route_weight.T).T


def solution(mesh):
    shape = mesh.devices.shape
    split = Mesh(mesh.devices.reshape(shape[:2] + (shape[2] // 2, 2)), ("dp", "node", "y", "core"))
    rows, cols = ("dp", "node"), ("y", "core")
    return jax.shard_map(
        local,
        mesh=split,
        in_specs=(
            P(rows, cols),
            P(rows, None),
            P(rows, None),
            P("node", None, cols),
            P("node", None, cols),
            P("node", None, cols),
        ),
        out_specs=P(rows, cols),
        check_vma=False,
    )
```

```python
import functools

import jax
import jax.numpy as jnp
from jax import lax
from jax.experimental import pallas as pl
from jax.experimental.pallas import tpu as pltpu
from jax.sharding import Mesh, PartitionSpec as P

F32, BF16 = jnp.float32, jnp.bfloat16
SWAP = [(0, 1), (1, 0)]
VMEM_LIMIT = 52 * 1024 * 1024
LAST_LIMIT = 32 * 1024 * 1024
NT = (((1,), (1,)), ((), ()))
TN = (((0,), (0,)), ((), ()))


def whole(shape):
    return pl.BlockSpec(shape, lambda i: (0,) * len(shape))


def dispatch_kernel(core_ref, own_ref, other_ref, routes_ref, rows_ref, pick_ref, both):
    width, count = own_ref.shape
    nodes, half, _ = rows_ref.shape
    core = core_ref[0]
    both[pl.ds(pl.multiple_of(core * width, width), width), :] = own_ref[...]
    both[pl.ds(pl.multiple_of((1 - core) * width, width), width), :] = other_ref[...]
    first, second = routes_ref[0:1, :], routes_ref[1:2, :]
    experts = lax.broadcasted_iota(jnp.int32, (8, count), 0)
    member = (first == experts) | (second == experts)
    before = lax.broadcasted_iota(jnp.int32, (count, count), 0)
    after = lax.broadcasted_iota(jnp.int32, (count, count), 1)
    slots = jnp.dot(
        member.astype(F32).astype(BF16),
        (before < after).astype(F32).astype(BF16),
        preferred_element_type=F32,
    ).astype(jnp.int32)
    for k, route in enumerate((first, second)):
        slot = jnp.sum(jnp.where(route == experts, slots, 0), axis=0, keepdims=True)
        pick_ref[k : k + 1, :] = route * (2 * half) + slot
    wanted = lax.broadcasted_iota(jnp.int32, (half, count), 0) + core * half
    for e in range(nodes):
        chosen = (first == e) | (second == e)
        place = jnp.where(chosen, slots[e : e + 1, :], -1)
        picker = (wanted == place).astype(F32).astype(BF16)
        rows_ref[e] = lax.dot_general(picker, both[...], NT, preferred_element_type=F32).astype(BF16)


def dispatch(core, own, other, routes, nodes, half):
    width, count = own.shape
    return pl.pallas_call(
        dispatch_kernel,
        out_shape=(
            jax.ShapeDtypeStruct((nodes, half, 2 * width), BF16),
            jax.ShapeDtypeStruct((2, count), jnp.int32),
        ),
        grid=(1,),
        in_specs=[pl.BlockSpec(memory_space=pltpu.SMEM)] + [whole(x.shape) for x in (own, other, routes)],
        out_specs=(whole((nodes, half, 2 * width)), whole((2, count))),
        scratch_shapes=[pltpu.VMEM((2 * width, count), BF16)],
        compiler_params=pltpu.CompilerParams(vmem_limit_bytes=VMEM_LIMIT),
        cost_estimate=pl.CostEstimate(flops=2 * nodes * half * count * 2 * width, bytes_accessed=2000000, transcendentals=0),
    )(core, own, other, routes)


def gate_up_kernel(layout, rest, last, idx_ref, *refs):
    refs = list(refs)
    x = []
    for parts in layout:
        x.append(jnp.concatenate([refs.pop(0)[...] for _ in range(parts)], axis=0))
    w = []
    for _ in layout:
        w.append(jnp.concatenate([refs.pop(0)[...] for _ in range(4)], axis=1))
    total = jnp.dot(jnp.concatenate(x, axis=1), jnp.concatenate(w, axis=0), preferred_element_type=F32)
    if rest:
        total = total + refs.pop(0)[...]
    out = refs.pop(0)
    if not last:
        out[...] = total
        return
    core = idx_ref[idx_ref.shape[0] - 1]
    hid = total.shape[1] // 4
    gate, up = total[:, :hid], total[:, hid : 2 * hid]
    own = gate / (1.0 + jnp.exp(-gate)) * up
    gate, up = total[:, 2 * hid : 3 * hid], total[:, 3 * hid :]
    other = gate / (1.0 + jnp.exp(-gate)) * up
    left = jnp.where(core == 0, own, other).astype(BF16)
    right = jnp.where(core == 0, other, own).astype(BF16)
    for k in range(out.shape[0]):
        out[k, :, :hid] = left
        out[k, :, hid:] = right


def gate_up(items, sums, weights, idx, last=None):
    operands = [b for blocks, _ in items for b in blocks]
    rows = sum(b.shape[0] for b in items[0][0])
    width, hid = operands[0].shape[1], weights[0].shape[1]
    full = lambda shape: pl.BlockSpec(shape, lambda i, idx: (0,) * len(shape))
    in_specs = [full(b.shape) for b in operands]
    for _, at in items:
        for w in weights:
            in_specs.append(pl.BlockSpec((width, hid), functools.partial(lambda at, i, idx: (idx[at], 0), at)))
            operands.append(w)
    aliases = {}
    if sums is not None:
        if last is None:
            aliases[1 + len(operands)] = 0
        in_specs.append(full(sums.shape))
        operands.append(sums)
    shape = jax.ShapeDtypeStruct((rows, 4 * hid), F32)
    if last is not None:
        shape = jax.ShapeDtypeStruct((last, rows, 2 * hid), BF16)
    return pl.pallas_call(
        functools.partial(
            gate_up_kernel, tuple(len(blocks) for blocks, _ in items), sums is not None, last is not None
        ),
        grid_spec=pltpu.PrefetchScalarGridSpec(
            num_scalar_prefetch=1, grid=(1,), in_specs=in_specs, out_specs=full(shape.shape)
        ),
        out_shape=shape,
        input_output_aliases=aliases,
        compiler_params=pltpu.CompilerParams(vmem_limit_bytes=VMEM_LIMIT if last is None else LAST_LIMIT),
        cost_estimate=pl.CostEstimate(
            flops=8 * len(items) * rows * width * hid,
            bytes_accessed=len(items) * width * (8 * hid + 2 * rows) + 16 * rows * hid,
            transcendentals=0,
        ),
    )(idx, *operands)


def down_kernel(core_ref, hidden_ref, own_ref, other_ref, out_ref, total):
    k = pl.program_id(0)
    hidden = jnp.concatenate([hidden_ref[j] for j in range(hidden_ref.shape[0])], axis=1)
    w = jnp.concatenate([own_ref[...], other_ref[...]], axis=0)
    part = lax.dot_general(hidden, w, NT, preferred_element_type=F32)

    @pl.when(k == 0)
    def _():
        total[...] = part

    @pl.when(k > 0)
    def _():
        nodes, _, half, width = out_ref.shape
        core = core_ref[0]
        for side, at in ((core, 0), (1 - core, width)):
            for e in range(nodes):
                rows, cols = slice(e * half, (e + 1) * half), slice(at, at + width)
                out_ref[e, side] = (total[rows, cols] + part[rows, cols]).astype(BF16)


def down(core, hidden, own, other, half):
    chips, rows, depth = hidden.shape
    width = own.shape[0]
    nodes = rows // half
    step = chips // 2
    return pl.pallas_call(
        down_kernel,
        grid=(2,),
        out_shape=jax.ShapeDtypeStruct((nodes, 2, half, width), BF16),
        in_specs=[
            pl.BlockSpec(memory_space=pltpu.SMEM),
            pl.BlockSpec((step, rows, depth), lambda k: (k, 0, 0)),
            pl.BlockSpec((width, step * depth), lambda k: (0, k)),
            pl.BlockSpec((width, step * depth), lambda k: (0, k)),
        ],
        out_specs=pl.BlockSpec((nodes, 2, half, width), lambda k: (0, 0, 0, 0)),
        scratch_shapes=[pltpu.VMEM((rows, 2 * width), F32)],
        compiler_params=pltpu.CompilerParams(vmem_limit_bytes=VMEM_LIMIT),
        cost_estimate=pl.CostEstimate(flops=4 * rows * depth * chips * width, bytes_accessed=6000000, transcendentals=0),
    )(core, hidden, own, other)


def combine_kernel(rows_ref, pick_ref, weight_ref, out_ref):
    total = rows_ref.shape[0]
    count = pick_ref.shape[1]
    row = lax.broadcasted_iota(jnp.int32, (total, count), 0)
    scale = jnp.zeros((total, count), F32)
    for k in range(pick_ref.shape[0]):
        scale = jnp.where(row == pick_ref[k : k + 1, :], weight_ref[k : k + 1, :], scale)
    high = scale.astype(BF16)
    low = (scale - high.astype(F32)).astype(BF16)
    rows = rows_ref[...]
    mixed = lax.dot_general(rows, high, TN, preferred_element_type=F32)
    mixed = mixed + lax.dot_general(rows, low, TN, preferred_element_type=F32)
    out_ref[...] = mixed.astype(BF16)


def combine(rows, pick, weight):
    total, width = rows.shape
    count = pick.shape[1]
    return pl.pallas_call(
        combine_kernel,
        out_shape=jax.ShapeDtypeStruct((width, count), BF16),
        grid=(1,),
        in_specs=[whole(x.shape) for x in (rows, pick, weight)],
        out_specs=whole((width, count)),
        compiler_params=pltpu.CompilerParams(vmem_limit_bytes=VMEM_LIMIT),
        cost_estimate=pl.CostEstimate(flops=4 * total * count * width, bytes_accessed=1500000, transcendentals=0),
    )(rows, pick, weight)


def local(tokens, routes, route_weight, w_gate, w_up, w_down):
    nodes, chips = lax.axis_size("node"), lax.axis_size("y")
    count, width = tokens.shape
    capacity = min(count, 5 * count * routes.shape[1] // (4 * nodes))
    half = capacity // 2
    core, here = lax.axis_index("core").astype(jnp.int32)[None], lax.axis_index("y")
    idx = jnp.concatenate([lax.rem(here + jnp.arange(chips), chips).astype(jnp.int32), core])

    def hop(x, distance):
        return lax.ppermute(x, "y", [(i, (i + distance) % chips) for i in range(chips)])

    def across(x):
        return lax.ppermute(x, "core", SWAP)

    def exchange(x, axes):
        return lax.all_to_all(x, axes, split_axis=0, concat_axis=0, tiled=True)

    own = tokens.T
    rows, pick = dispatch(core, own, across(own), routes.T, nodes, half)
    size = nodes * half
    gate_w, up_w, rows = lax.optimization_barrier((w_gate[0], w_up[0], rows))
    rows = exchange(rows, "node").reshape(size, 2 * width)
    weights = (gate_w, up_w, across(gate_w), across(up_w))

    up_y, down_y = hop(rows, 1), hop(rows, -1)
    sums = gate_up([((rows,), 0), ((up_y,), chips - 1), ((down_y,), 1)], None, weights, idx)
    for s in range(2, chips // 2):
        up_y, down_y = hop(up_y, 1), hop(down_y, -1)
        new = gate_up([((up_y,), chips - s), ((down_y,), s)], sums, weights, idx)
        up_y, down_y, sums = lax.optimization_barrier((up_y, down_y, sums))
        sums = new
    pairs = [(y, side) for y in range(chips) for side in range(2)]
    pairs = [(2 * y + side, 2 * ((y + 1 - 2 * side) % chips) + side) for y, side in pairs]
    far = lax.ppermute(jnp.where(core[0] == 0, up_y, down_y), ("y", "core"), pairs)
    hidden = gate_up([((far,), chips // 2)], sums, weights, idx, last=chips)
    hidden, down_w = lax.optimization_barrier((hidden, w_down[0].T))
    hidden, down_other = exchange(hidden, "y"), across(down_w)
    out = down(core, hidden, down_w, down_other, half)
    back = exchange(out.reshape(2 * nodes, half, width), ("node", "core"))
    return combine(back.reshape(2 * nodes * half, width), pick, route_weight.T).T


def solution(mesh):
    shape = mesh.devices.shape
    split = Mesh(mesh.devices.reshape(shape[:2] + (shape[2] // 2, 2)), ("dp", "node", "y", "core"))
    rows, cols = ("dp", "node"), ("y", "core")
    return jax.shard_map(
        local,
        mesh=split,
        in_specs=(
            P(rows, cols),
            P(rows, None),
            P(rows, None),
            P("node", None, cols),
            P("node", None, cols),
            P("node", None, cols),
        ),
        out_specs=P(rows, cols),
        check_vma=False,
    )
```

```python
import functools

import jax
import jax.numpy as jnp
from jax import lax
from jax.experimental import pallas as pl
from jax.experimental.pallas import tpu as pltpu
from jax.sharding import Mesh, PartitionSpec as P

F32, BF16 = jnp.float32, jnp.bfloat16
SWAP = [(0, 1), (1, 0)]
VMEM_LIMIT = 52 * 1024 * 1024
LAST_LIMIT = 32 * 1024 * 1024
NT = (((1,), (1,)), ((), ()))
TN = (((0,), (0,)), ((), ()))


def whole(shape):
    return pl.BlockSpec(shape, lambda i: (0,) * len(shape))


def dispatch_kernel(core_ref, own_ref, other_ref, routes_ref, rows_ref, pick_ref, both):
    width, count = own_ref.shape
    nodes, half, _ = rows_ref.shape
    core = core_ref[0]
    both[pl.ds(pl.multiple_of(core * width, width), width), :] = own_ref[...]
    both[pl.ds(pl.multiple_of((1 - core) * width, width), width), :] = other_ref[...]
    first, second = routes_ref[0:1, :], routes_ref[1:2, :]
    experts = lax.broadcasted_iota(jnp.int32, (8, count), 0)
    member = (first == experts) | (second == experts)
    before = lax.broadcasted_iota(jnp.int32, (count, count), 0)
    after = lax.broadcasted_iota(jnp.int32, (count, count), 1)
    slots = jnp.dot(
        member.astype(F32).astype(BF16),
        (before < after).astype(F32).astype(BF16),
        preferred_element_type=F32,
    ).astype(jnp.int32)
    for k, route in enumerate((first, second)):
        slot = jnp.sum(jnp.where(route == experts, slots, 0), axis=0, keepdims=True)
        pick_ref[k : k + 1, :] = route * (2 * half) + slot
    wanted = lax.broadcasted_iota(jnp.int32, (half, count), 0) + core * half
    for e in range(nodes):
        chosen = (first == e) | (second == e)
        place = jnp.where(chosen, slots[e : e + 1, :], -1)
        picker = (wanted == place).astype(F32).astype(BF16)
        rows_ref[e] = lax.dot_general(picker, both[...], NT, preferred_element_type=F32).astype(BF16)


def dispatch(core, own, other, routes, nodes, half):
    width, count = own.shape
    return pl.pallas_call(
        dispatch_kernel,
        out_shape=(
            jax.ShapeDtypeStruct((nodes, half, 2 * width), BF16),
            jax.ShapeDtypeStruct((2, count), jnp.int32),
        ),
        grid=(1,),
        in_specs=[pl.BlockSpec(memory_space=pltpu.SMEM)] + [whole(x.shape) for x in (own, other, routes)],
        out_specs=(whole((nodes, half, 2 * width)), whole((2, count))),
        scratch_shapes=[pltpu.VMEM((2 * width, count), BF16)],
        compiler_params=pltpu.CompilerParams(vmem_limit_bytes=VMEM_LIMIT),
        cost_estimate=pl.CostEstimate(flops=2 * nodes * half * count * 2 * width, bytes_accessed=2000000, transcendentals=0),
    )(core, own, other, routes)


def gate_up_kernel(layout, rest, last, idx_ref, *refs):
    refs = list(refs)
    x = []
    for parts in layout:
        x.append(jnp.concatenate([refs.pop(0)[...] for _ in range(parts)], axis=0))
    w = []
    for _ in layout:
        w.append(jnp.concatenate([refs.pop(0)[...] for _ in range(4)], axis=1))
    total = jnp.dot(jnp.concatenate(x, axis=1), jnp.concatenate(w, axis=0), preferred_element_type=F32)
    if rest:
        total = total + refs.pop(0)[...]
    out = refs.pop(0)
    if not last:
        out[...] = total
        return
    core = idx_ref[idx_ref.shape[0] - 1]
    hid = total.shape[1] // 4
    gate, up = total[:, :hid], total[:, hid : 2 * hid]
    own = gate / (1.0 + jnp.exp(-gate)) * up
    gate, up = total[:, 2 * hid : 3 * hid], total[:, 3 * hid :]
    other = gate / (1.0 + jnp.exp(-gate)) * up
    left = jnp.where(core == 0, own, other).astype(BF16)
    right = jnp.where(core == 0, other, own).astype(BF16)
    for k in range(out.shape[0]):
        out[k, :, :hid] = left
        out[k, :, hid:] = right


def gate_up(items, sums, weights, idx, last=None):
    operands = [b for blocks, _ in items for b in blocks]
    rows = sum(b.shape[0] for b in items[0][0])
    width, hid = operands[0].shape[1], weights[0].shape[1]
    full = lambda shape: pl.BlockSpec(shape, lambda i, idx: (0,) * len(shape))
    in_specs = [full(b.shape) for b in operands]
    for _, at in items:
        for w in weights:
            in_specs.append(pl.BlockSpec((width, hid), functools.partial(lambda at, i, idx: (idx[at], 0), at)))
            operands.append(w)
    aliases = {}
    if sums is not None:
        if last is None:
            aliases[1 + len(operands)] = 0
        in_specs.append(full(sums.shape))
        operands.append(sums)
    shape = jax.ShapeDtypeStruct((rows, 4 * hid), F32)
    if last is not None:
        shape = jax.ShapeDtypeStruct((last, rows, 2 * hid), BF16)
    return pl.pallas_call(
        functools.partial(
            gate_up_kernel, tuple(len(blocks) for blocks, _ in items), sums is not None, last is not None
        ),
        grid_spec=pltpu.PrefetchScalarGridSpec(
            num_scalar_prefetch=1, grid=(1,), in_specs=in_specs, out_specs=full(shape.shape)
        ),
        out_shape=shape,
        input_output_aliases=aliases,
        compiler_params=pltpu.CompilerParams(vmem_limit_bytes=VMEM_LIMIT if last is None else LAST_LIMIT),
        cost_estimate=pl.CostEstimate(
            flops=8 * len(items) * rows * width * hid,
            bytes_accessed=len(items) * width * (8 * hid + 2 * rows) + 16 * rows * hid,
            transcendentals=0,
        ),
    )(idx, *operands)


def down_kernel(core_ref, hidden_ref, own_ref, other_ref, out_ref, total):
    k = pl.program_id(0)
    hidden = jnp.concatenate([hidden_ref[j] for j in range(hidden_ref.shape[0])], axis=1)
    w = jnp.concatenate([own_ref[...], other_ref[...]], axis=0)
    part = lax.dot_general(hidden, w, NT, preferred_element_type=F32)

    @pl.when(k == 0)
    def _():
        total[...] = part

    @pl.when(k > 0)
    def _():
        nodes, _, half, width = out_ref.shape
        core = core_ref[0]
        for side, at in ((core, 0), (1 - core, width)):
            for e in range(nodes):
                rows, cols = slice(e * half, (e + 1) * half), slice(at, at + width)
                out_ref[e, side] = (total[rows, cols] + part[rows, cols]).astype(BF16)


def down(core, hidden, own, other, half):
    chips, rows, depth = hidden.shape
    width = own.shape[0]
    nodes = rows // half
    step = chips // 2
    return pl.pallas_call(
        down_kernel,
        grid=(2,),
        out_shape=jax.ShapeDtypeStruct((nodes, 2, half, width), BF16),
        in_specs=[
            pl.BlockSpec(memory_space=pltpu.SMEM),
            pl.BlockSpec((step, rows, depth), lambda k: (k, 0, 0)),
            pl.BlockSpec((width, step * depth), lambda k: (0, k)),
            pl.BlockSpec((width, step * depth), lambda k: (0, k)),
        ],
        out_specs=pl.BlockSpec((nodes, 2, half, width), lambda k: (0, 0, 0, 0)),
        scratch_shapes=[pltpu.VMEM((rows, 2 * width), F32)],
        compiler_params=pltpu.CompilerParams(vmem_limit_bytes=VMEM_LIMIT),
        cost_estimate=pl.CostEstimate(flops=4 * rows * depth * chips * width, bytes_accessed=6000000, transcendentals=0),
    )(core, hidden, own, other)


def combine_kernel(rows_ref, pick_ref, weight_ref, out_ref):
    total = rows_ref.shape[0]
    count = pick_ref.shape[1]
    row = lax.broadcasted_iota(jnp.int32, (total, count), 0)
    scale = jnp.zeros((total, count), F32)
    for k in range(pick_ref.shape[0]):
        scale = jnp.where(row == pick_ref[k : k + 1, :], weight_ref[k : k + 1, :], scale)
    high = scale.astype(BF16)
    low = (scale - high.astype(F32)).astype(BF16)
    rows = rows_ref[...]
    mixed = lax.dot_general(rows, high, TN, preferred_element_type=F32)
    mixed = mixed + lax.dot_general(rows, low, TN, preferred_element_type=F32)
    out_ref[...] = mixed.astype(BF16)


def combine(rows, pick, weight):
    total, width = rows.shape
    count = pick.shape[1]
    return pl.pallas_call(
        combine_kernel,
        out_shape=jax.ShapeDtypeStruct((width, count), BF16),
        grid=(1,),
        in_specs=[whole(x.shape) for x in (rows, pick, weight)],
        out_specs=whole((width, count)),
        compiler_params=pltpu.CompilerParams(vmem_limit_bytes=VMEM_LIMIT),
        cost_estimate=pl.CostEstimate(flops=4 * total * count * width, bytes_accessed=1500000, transcendentals=0),
    )(rows, pick, weight)


def local(tokens, routes, route_weight, w_gate, w_up, w_down):
    nodes, chips = lax.axis_size("node"), lax.axis_size("y")
    count, width = tokens.shape
    capacity = min(count, 5 * count * routes.shape[1] // (4 * nodes))
    half = capacity // 2
    core, here = lax.axis_index("core").astype(jnp.int32)[None], lax.axis_index("y")
    idx = jnp.concatenate([lax.rem(here + jnp.arange(chips), chips).astype(jnp.int32), core])

    def hop(x, distance):
        return lax.ppermute(x, "y", [(i, (i + distance) % chips) for i in range(chips)])

    def across(x):
        return lax.ppermute(x, "core", SWAP)

    def exchange(x, axes):
        return lax.all_to_all(x, axes, split_axis=0, concat_axis=0, tiled=True)

    own = tokens.T
    rows, pick = dispatch(core, own, across(own), routes.T, nodes, half)
    size = nodes * half
    gate_w, up_w, rows = lax.optimization_barrier((w_gate[0], w_up[0], rows))
    rows = exchange(rows, "node").reshape(size, 2 * width)
    weights = (gate_w, up_w, across(gate_w), across(up_w))

    up_y, down_y = hop(rows, 1), hop(rows, -1)
    sums = gate_up([((rows,), 0), ((up_y,), chips - 1), ((down_y,), 1)], None, weights, idx)
    for s in range(2, chips // 2):
        up_y, down_y = hop(up_y, 1), hop(down_y, -1)
        new = gate_up([((up_y,), chips - s), ((down_y,), s)], sums, weights, idx)
        down_y, sums = lax.optimization_barrier((down_y, sums))
        sums = new
    pairs = [(y, side) for y in range(chips) for side in range(2)]
    pairs = [(2 * y + side, 2 * ((y + 1 - 2 * side) % chips) + side) for y, side in pairs]
    far = lax.ppermute(jnp.where(core[0] == 0, up_y, down_y), ("y", "core"), pairs)
    hidden = gate_up([((far,), chips // 2)], sums, weights, idx, last=chips)
    hidden, down_w = lax.optimization_barrier((hidden, w_down[0].T))
    hidden, down_other = exchange(hidden, "y"), across(down_w)
    out = down(core, hidden, down_w, down_other, half)
    back = exchange(out.reshape(2 * nodes, half, width), ("node", "core"))
    return combine(back.reshape(2 * nodes * half, width), pick, route_weight.T).T


def solution(mesh):
    shape = mesh.devices.shape
    split = Mesh(mesh.devices.reshape(shape[:2] + (shape[2] // 2, 2)), ("dp", "node", "y", "core"))
    rows, cols = ("dp", "node"), ("y", "core")
    return jax.shard_map(
        local,
        mesh=split,
        in_specs=(
            P(rows, cols),
            P(rows, None),
            P(rows, None),
            P("node", None, cols),
            P("node", None, cols),
            P("node", None, cols),
        ),
        out_specs=P(rows, cols),
        check_vma=False,
    )
```

```python
import functools

import jax
import jax.numpy as jnp
from jax import lax
from jax.experimental import pallas as pl
from jax.experimental.pallas import tpu as pltpu
from jax.sharding import Mesh, PartitionSpec as P

F32, BF16 = jnp.float32, jnp.bfloat16
SWAP = [(0, 1), (1, 0)]
VMEM_LIMIT = 52 * 1024 * 1024
LAST_LIMIT = 32 * 1024 * 1024
NT = (((1,), (1,)), ((), ()))
TN = (((0,), (0,)), ((), ()))


def whole(shape):
    return pl.BlockSpec(shape, lambda i: (0,) * len(shape))


def dispatch_kernel(core_ref, own_ref, other_ref, routes_ref, rows_ref, pick_ref, both):
    width, count = own_ref.shape
    nodes, half, _ = rows_ref.shape
    core = core_ref[0]
    both[pl.ds(pl.multiple_of(core * width, width), width), :] = own_ref[...]
    both[pl.ds(pl.multiple_of((1 - core) * width, width), width), :] = other_ref[...]
    first, second = routes_ref[0:1, :], routes_ref[1:2, :]
    experts = lax.broadcasted_iota(jnp.int32, (8, count), 0)
    member = (first == experts) | (second == experts)
    before = lax.broadcasted_iota(jnp.int32, (count, count), 0)
    after = lax.broadcasted_iota(jnp.int32, (count, count), 1)
    slots = jnp.dot(
        member.astype(F32).astype(BF16),
        (before < after).astype(F32).astype(BF16),
        preferred_element_type=F32,
    ).astype(jnp.int32)
    for k, route in enumerate((first, second)):
        slot = jnp.sum(jnp.where(route == experts, slots, 0), axis=0, keepdims=True)
        pick_ref[k : k + 1, :] = route * (2 * half) + slot
    wanted = lax.broadcasted_iota(jnp.int32, (half, count), 0) + core * half
    for e in range(nodes):
        chosen = (first == e) | (second == e)
        place = jnp.where(chosen, slots[e : e + 1, :], -1)
        picker = (wanted == place).astype(F32).astype(BF16)
        rows_ref[e] = lax.dot_general(picker, both[...], NT, preferred_element_type=F32).astype(BF16)


def dispatch(core, own, other, routes, nodes, half):
    width, count = own.shape
    return pl.pallas_call(
        dispatch_kernel,
        out_shape=(
            jax.ShapeDtypeStruct((nodes, half, 2 * width), BF16),
            jax.ShapeDtypeStruct((2, count), jnp.int32),
        ),
        grid=(1,),
        in_specs=[pl.BlockSpec(memory_space=pltpu.SMEM)] + [whole(x.shape) for x in (own, other, routes)],
        out_specs=(whole((nodes, half, 2 * width)), whole((2, count))),
        scratch_shapes=[pltpu.VMEM((2 * width, count), BF16)],
        compiler_params=pltpu.CompilerParams(vmem_limit_bytes=VMEM_LIMIT),
        cost_estimate=pl.CostEstimate(flops=2 * nodes * half * count * 2 * width, bytes_accessed=2000000, transcendentals=0),
    )(core, own, other, routes)


def gate_up_kernel(layout, rest, last, idx_ref, *refs):
    refs = list(refs)
    x = []
    for parts in layout:
        x.append(jnp.concatenate([refs.pop(0)[...] for _ in range(parts)], axis=0))
    w = []
    for _ in layout:
        w.append(jnp.concatenate([refs.pop(0)[...] for _ in range(4)], axis=1))
    total = jnp.dot(jnp.concatenate(x, axis=1), jnp.concatenate(w, axis=0), preferred_element_type=F32)
    if rest:
        total = total + refs.pop(0)[...]
    out = refs.pop(0)
    if not last:
        out[...] = total
        return
    core = idx_ref[idx_ref.shape[0] - 1]
    hid = total.shape[1] // 4
    gate, up = total[:, :hid], total[:, hid : 2 * hid]
    own = gate / (1.0 + jnp.exp(-gate)) * up
    gate, up = total[:, 2 * hid : 3 * hid], total[:, 3 * hid :]
    other = gate / (1.0 + jnp.exp(-gate)) * up
    left = jnp.where(core == 0, own, other).astype(BF16)
    right = jnp.where(core == 0, other, own).astype(BF16)
    for k in range(out.shape[0]):
        out[k, :, :hid] = left
        out[k, :, hid:] = right


def gate_up(items, sums, weights, idx, last=None):
    operands = [b for blocks, _ in items for b in blocks]
    rows = sum(b.shape[0] for b in items[0][0])
    width, hid = operands[0].shape[1], weights[0].shape[1]
    full = lambda shape: pl.BlockSpec(shape, lambda i, idx: (0,) * len(shape))
    in_specs = [full(b.shape) for b in operands]
    for _, at in items:
        for w in weights:
            in_specs.append(pl.BlockSpec((width, hid), functools.partial(lambda at, i, idx: (idx[at], 0), at)))
            operands.append(w)
    aliases = {}
    if sums is not None:
        if last is None:
            aliases[1 + len(operands)] = 0
        in_specs.append(full(sums.shape))
        operands.append(sums)
    shape = jax.ShapeDtypeStruct((rows, 4 * hid), F32)
    if last is not None:
        shape = jax.ShapeDtypeStruct((last, rows, 2 * hid), BF16)
    return pl.pallas_call(
        functools.partial(
            gate_up_kernel, tuple(len(blocks) for blocks, _ in items), sums is not None, last is not None
        ),
        grid_spec=pltpu.PrefetchScalarGridSpec(
            num_scalar_prefetch=1, grid=(1,), in_specs=in_specs, out_specs=full(shape.shape)
        ),
        out_shape=shape,
        input_output_aliases=aliases,
        compiler_params=pltpu.CompilerParams(vmem_limit_bytes=VMEM_LIMIT if last is None else LAST_LIMIT),
        cost_estimate=pl.CostEstimate(
            flops=8 * len(items) * rows * width * hid,
            bytes_accessed=len(items) * width * (8 * hid + 2 * rows) + 16 * rows * hid,
            transcendentals=0,
        ),
    )(idx, *operands)


def down_kernel(core_ref, hidden_ref, own_ref, other_ref, out_ref, total):
    k = pl.program_id(0)
    hidden = jnp.concatenate([hidden_ref[j] for j in range(hidden_ref.shape[0])], axis=1)
    w = jnp.concatenate([own_ref[...], other_ref[...]], axis=0)
    part = lax.dot_general(hidden, w, NT, preferred_element_type=F32)

    @pl.when(k == 0)
    def _():
        total[...] = part

    @pl.when(k > 0)
    def _():
        nodes, _, half, width = out_ref.shape
        core = core_ref[0]
        for side, at in ((core, 0), (1 - core, width)):
            for e in range(nodes):
                rows, cols = slice(e * half, (e + 1) * half), slice(at, at + width)
                out_ref[e, side] = (total[rows, cols] + part[rows, cols]).astype(BF16)


def down(core, hidden, own, other, half):
    chips, rows, depth = hidden.shape
    width = own.shape[0]
    nodes = rows // half
    step = chips // 2
    return pl.pallas_call(
        down_kernel,
        grid=(2,),
        out_shape=jax.ShapeDtypeStruct((nodes, 2, half, width), BF16),
        in_specs=[
            pl.BlockSpec(memory_space=pltpu.SMEM),
            pl.BlockSpec((step, rows, depth), lambda k: (k, 0, 0)),
            pl.BlockSpec((width, step * depth), lambda k: (0, k)),
            pl.BlockSpec((width, step * depth), lambda k: (0, k)),
        ],
        out_specs=pl.BlockSpec((nodes, 2, half, width), lambda k: (0, 0, 0, 0)),
        scratch_shapes=[pltpu.VMEM((rows, 2 * width), F32)],
        compiler_params=pltpu.CompilerParams(vmem_limit_bytes=VMEM_LIMIT),
        cost_estimate=pl.CostEstimate(flops=4 * rows * depth * chips * width, bytes_accessed=6000000, transcendentals=0),
    )(core, hidden, own, other)


def combine_kernel(rows_ref, pick_ref, weight_ref, out_ref):
    total = rows_ref.shape[0]
    count = pick_ref.shape[1]
    row = lax.broadcasted_iota(jnp.int32, (total, count), 0)
    scale = jnp.zeros((total, count), F32)
    for k in range(pick_ref.shape[0]):
        scale = jnp.where(row == pick_ref[k : k + 1, :], weight_ref[k : k + 1, :], scale)
    high = scale.astype(BF16)
    low = (scale - high.astype(F32)).astype(BF16)
    rows = rows_ref[...]
    mixed = lax.dot_general(rows, high, TN, preferred_element_type=F32)
    mixed = mixed + lax.dot_general(rows, low, TN, preferred_element_type=F32)
    out_ref[...] = mixed.astype(BF16)


def combine(rows, pick, weight):
    total, width = rows.shape
    count = pick.shape[1]
    return pl.pallas_call(
        combine_kernel,
        out_shape=jax.ShapeDtypeStruct((width, count), BF16),
        grid=(1,),
        in_specs=[whole(x.shape) for x in (rows, pick, weight)],
        out_specs=whole((width, count)),
        compiler_params=pltpu.CompilerParams(vmem_limit_bytes=VMEM_LIMIT),
        cost_estimate=pl.CostEstimate(flops=4 * total * count * width, bytes_accessed=1500000, transcendentals=0),
    )(rows, pick, weight)


def local(tokens, routes, route_weight, w_gate, w_up, w_down):
    nodes, chips = lax.axis_size("node"), lax.axis_size("y")
    count, width = tokens.shape
    capacity = min(count, 5 * count * routes.shape[1] // (4 * nodes))
    half = capacity // 2
    core, here = lax.axis_index("core").astype(jnp.int32)[None], lax.axis_index("y")
    idx = jnp.concatenate([lax.rem(here + jnp.arange(chips), chips).astype(jnp.int32), core])

    def hop(x, distance):
        return lax.ppermute(x, "y", [(i, (i + distance) % chips) for i in range(chips)])

    def across(x):
        return lax.ppermute(x, "core", SWAP)

    def exchange(x, axes):
        return lax.all_to_all(x, axes, split_axis=0, concat_axis=0, tiled=True)

    own = tokens.T
    rows, pick = dispatch(core, own, across(own), routes.T, nodes, half)
    size = nodes * half
    gate_w, up_w, rows = lax.optimization_barrier((w_gate[0], w_up[0], rows))
    rows = exchange(rows, "node").reshape(size, 2 * width)
    weights = (gate_w, up_w, across(gate_w), across(up_w))

    up_y, down_y = hop(rows, 1), hop(rows, -1)
    sums = gate_up([((rows,), 0), ((up_y,), chips - 1), ((down_y,), 1)], None, weights, idx)
    far = None
    for s in range(2, chips // 2):
        up_y, down_y = hop(up_y, 1), hop(down_y, -1)
        new = gate_up([((up_y,), chips - s), ((down_y,), s)], sums, weights, idx)
        if s == chips // 2 - 2:
            pairs = [(y, side) for y in range(chips) for side in range(2)]
            pairs = [(2 * y + side, 2 * ((y + 2 - 4 * side) % chips) + side) for y, side in pairs]
            far = lax.ppermute(jnp.where(core[0] == 0, up_y, down_y), ("y", "core"), pairs)
            down_y, sums = lax.optimization_barrier((down_y, sums))
        sums = new
    hidden = gate_up([((far,), chips // 2)], sums, weights, idx, last=chips)
    hidden, down_w = lax.optimization_barrier((hidden, w_down[0].T))
    hidden, down_other = exchange(hidden, "y"), across(down_w)
    out = down(core, hidden, down_w, down_other, half)
    back = exchange(out.reshape(2 * nodes, half, width), ("node", "core"))
    return combine(back.reshape(2 * nodes * half, width), pick, route_weight.T).T


def solution(mesh):
    shape = mesh.devices.shape
    split = Mesh(mesh.devices.reshape(shape[:2] + (shape[2] // 2, 2)), ("dp", "node", "y", "core"))
    rows, cols = ("dp", "node"), ("y", "core")
    return jax.shard_map(
        local,
        mesh=split,
        in_specs=(
            P(rows, cols),
            P(rows, None),
            P(rows, None),
            P("node", None, cols),
            P("node", None, cols),
            P("node", None, cols),
        ),
        out_specs=P(rows, cols),
        check_vma=False,
    )
```

```python
import functools

import jax
import jax.numpy as jnp
from jax import lax
from jax.experimental import pallas as pl
from jax.experimental.pallas import tpu as pltpu
from jax.sharding import Mesh, PartitionSpec as P

F32, BF16 = jnp.float32, jnp.bfloat16
SWAP = [(0, 1), (1, 0)]
VMEM_LIMIT = 52 * 1024 * 1024
LAST_LIMIT = 32 * 1024 * 1024
NT = (((1,), (1,)), ((), ()))
TN = (((0,), (0,)), ((), ()))


def whole(shape):
    return pl.BlockSpec(shape, lambda i: (0,) * len(shape))


def dispatch_kernel(core_ref, own_ref, other_ref, routes_ref, rows_ref, pick_ref, both):
    width, count = own_ref.shape
    nodes, half, _ = rows_ref.shape
    core = core_ref[0]
    both[pl.ds(pl.multiple_of(core * width, width), width), :] = own_ref[...]
    both[pl.ds(pl.multiple_of((1 - core) * width, width), width), :] = other_ref[...]
    first, second = routes_ref[0:1, :], routes_ref[1:2, :]
    experts = lax.broadcasted_iota(jnp.int32, (8, count), 0)
    member = (first == experts) | (second == experts)
    before = lax.broadcasted_iota(jnp.int32, (count, count), 0)
    after = lax.broadcasted_iota(jnp.int32, (count, count), 1)
    slots = jnp.dot(
        member.astype(F32).astype(BF16),
        (before < after).astype(F32).astype(BF16),
        preferred_element_type=F32,
    ).astype(jnp.int32)
    for k, route in enumerate((first, second)):
        slot = jnp.sum(jnp.where(route == experts, slots, 0), axis=0, keepdims=True)
        pick_ref[k : k + 1, :] = route * (2 * half) + slot
    wanted = lax.broadcasted_iota(jnp.int32, (half, count), 0) + core * half
    for e in range(nodes):
        chosen = (first == e) | (second == e)
        place = jnp.where(chosen, slots[e : e + 1, :], -1)
        picker = (wanted == place).astype(F32).astype(BF16)
        rows_ref[e] = lax.dot_general(picker, both[...], NT, preferred_element_type=F32).astype(BF16)


def dispatch(core, own, other, routes, nodes, half):
    width, count = own.shape
    return pl.pallas_call(
        dispatch_kernel,
        out_shape=(
            jax.ShapeDtypeStruct((nodes, half, 2 * width), BF16),
            jax.ShapeDtypeStruct((2, count), jnp.int32),
        ),
        grid=(1,),
        in_specs=[pl.BlockSpec(memory_space=pltpu.SMEM)] + [whole(x.shape) for x in (own, other, routes)],
        out_specs=(whole((nodes, half, 2 * width)), whole((2, count))),
        scratch_shapes=[pltpu.VMEM((2 * width, count), BF16)],
        compiler_params=pltpu.CompilerParams(vmem_limit_bytes=VMEM_LIMIT),
        cost_estimate=pl.CostEstimate(flops=2 * nodes * half * count * 2 * width, bytes_accessed=2000000, transcendentals=0),
    )(core, own, other, routes)


def gate_up_kernel(layout, rest, last, idx_ref, *refs):
    refs = list(refs)
    x = []
    for parts in layout:
        x.append(jnp.concatenate([refs.pop(0)[...] for _ in range(parts)], axis=0))
    w = []
    for _ in layout:
        w.append(jnp.concatenate([refs.pop(0)[...] for _ in range(4)], axis=1))
    total = jnp.dot(jnp.concatenate(x, axis=1), jnp.concatenate(w, axis=0), preferred_element_type=F32)
    if rest:
        total = total + refs.pop(0)[...]
    out = refs.pop(0)
    if not last:
        out[...] = total
        return
    core = idx_ref[idx_ref.shape[0] - 1]
    hid = total.shape[1] // 4
    gate, up = total[:, :hid], total[:, hid : 2 * hid]
    own = gate / (1.0 + jnp.exp(-gate)) * up
    gate, up = total[:, 2 * hid : 3 * hid], total[:, 3 * hid :]
    other = gate / (1.0 + jnp.exp(-gate)) * up
    left = jnp.where(core == 0, own, other).astype(BF16)
    right = jnp.where(core == 0, other, own).astype(BF16)
    for k in range(out.shape[0]):
        out[k, :, :hid] = left
        out[k, :, hid:] = right


def gate_up(items, sums, weights, idx, last=None):
    operands = [b for blocks, _ in items for b in blocks]
    rows = sum(b.shape[0] for b in items[0][0])
    width, hid = operands[0].shape[1], weights[0].shape[1]
    full = lambda shape: pl.BlockSpec(shape, lambda i, idx: (0,) * len(shape))
    in_specs = [full(b.shape) for b in operands]
    for _, at in items:
        for w in weights:
            in_specs.append(pl.BlockSpec((width, hid), functools.partial(lambda at, i, idx: (idx[at], 0), at)))
            operands.append(w)
    aliases = {}
    if sums is not None:
        if last is None:
            aliases[1 + len(operands)] = 0
        in_specs.append(full(sums.shape))
        operands.append(sums)
    shape = jax.ShapeDtypeStruct((rows, 4 * hid), F32)
    if last is not None:
        shape = jax.ShapeDtypeStruct((last, rows, 2 * hid), BF16)
    return pl.pallas_call(
        functools.partial(
            gate_up_kernel, tuple(len(blocks) for blocks, _ in items), sums is not None, last is not None
        ),
        grid_spec=pltpu.PrefetchScalarGridSpec(
            num_scalar_prefetch=1, grid=(1,), in_specs=in_specs, out_specs=full(shape.shape)
        ),
        out_shape=shape,
        input_output_aliases=aliases,
        compiler_params=pltpu.CompilerParams(vmem_limit_bytes=VMEM_LIMIT if last is None else LAST_LIMIT),
        cost_estimate=pl.CostEstimate(
            flops=8 * len(items) * rows * width * hid,
            bytes_accessed=len(items) * width * (8 * hid + 2 * rows) + 16 * rows * hid,
            transcendentals=0,
        ),
    )(idx, *operands)


def down_kernel(core_ref, hidden_ref, own_ref, other_ref, out_ref, total):
    k = pl.program_id(0)
    hidden = jnp.concatenate([hidden_ref[j] for j in range(hidden_ref.shape[0])], axis=1)
    w = jnp.concatenate([own_ref[...], other_ref[...]], axis=0)
    part = lax.dot_general(hidden, w, NT, preferred_element_type=F32)

    @pl.when(k == 0)
    def _():
        total[...] = part

    @pl.when(k > 0)
    def _():
        nodes, _, half, width = out_ref.shape
        core = core_ref[0]
        for side, at in ((core, 0), (1 - core, width)):
            for e in range(nodes):
                rows, cols = slice(e * half, (e + 1) * half), slice(at, at + width)
                out_ref[e, side] = (total[rows, cols] + part[rows, cols]).astype(BF16)


def down(core, hidden, own, other, half):
    chips, rows, depth = hidden.shape
    width = own.shape[0]
    nodes = rows // half
    step = chips // 2
    return pl.pallas_call(
        down_kernel,
        grid=(2,),
        out_shape=jax.ShapeDtypeStruct((nodes, 2, half, width), BF16),
        in_specs=[
            pl.BlockSpec(memory_space=pltpu.SMEM),
            pl.BlockSpec((step, rows, depth), lambda k: (k, 0, 0)),
            pl.BlockSpec((width, step * depth), lambda k: (0, k)),
            pl.BlockSpec((width, step * depth), lambda k: (0, k)),
        ],
        out_specs=pl.BlockSpec((nodes, 2, half, width), lambda k: (0, 0, 0, 0)),
        scratch_shapes=[pltpu.VMEM((rows, 2 * width), F32)],
        compiler_params=pltpu.CompilerParams(vmem_limit_bytes=VMEM_LIMIT),
        cost_estimate=pl.CostEstimate(flops=4 * rows * depth * chips * width, bytes_accessed=6000000, transcendentals=0),
    )(core, hidden, own, other)


def combine_kernel(rows_ref, pick_ref, weight_ref, out_ref):
    total = rows_ref.shape[0]
    count = pick_ref.shape[1]
    row = lax.broadcasted_iota(jnp.int32, (total, count), 0)
    scale = jnp.zeros((total, count), F32)
    for k in range(pick_ref.shape[0]):
        scale = jnp.where(row == pick_ref[k : k + 1, :], weight_ref[k : k + 1, :], scale)
    high = scale.astype(BF16)
    low = (scale - high.astype(F32)).astype(BF16)
    rows = rows_ref[...]
    mixed = lax.dot_general(rows, high, TN, preferred_element_type=F32)
    mixed = mixed + lax.dot_general(rows, low, TN, preferred_element_type=F32)
    out_ref[...] = mixed.astype(BF16)


def combine(rows, pick, weight):
    total, width = rows.shape
    count = pick.shape[1]
    return pl.pallas_call(
        combine_kernel,
        out_shape=jax.ShapeDtypeStruct((width, count), BF16),
        grid=(1,),
        in_specs=[whole(x.shape) for x in (rows, pick, weight)],
        out_specs=whole((width, count)),
        compiler_params=pltpu.CompilerParams(vmem_limit_bytes=VMEM_LIMIT),
        cost_estimate=pl.CostEstimate(flops=4 * total * count * width, bytes_accessed=1500000, transcendentals=0),
    )(rows, pick, weight)


def local(tokens, routes, route_weight, w_gate, w_up, w_down):
    nodes, chips = lax.axis_size("node"), lax.axis_size("y")
    count, width = tokens.shape
    capacity = min(count, 5 * count * routes.shape[1] // (4 * nodes))
    half = capacity // 2
    core, here = lax.axis_index("core").astype(jnp.int32)[None], lax.axis_index("y")
    idx = jnp.concatenate([lax.rem(here + jnp.arange(chips), chips).astype(jnp.int32), core])

    def hop(x, distance):
        return lax.ppermute(x, "y", [(i, (i + distance) % chips) for i in range(chips)])

    def across(x):
        return lax.ppermute(x, "core", SWAP)

    def exchange(x, axes):
        return lax.all_to_all(x, axes, split_axis=0, concat_axis=0, tiled=True)

    own = tokens.T
    rows, pick = dispatch(core, own, across(own), routes.T, nodes, half)
    size = nodes * half
    gate_w, up_w, rows = lax.optimization_barrier((w_gate[0], w_up[0], rows))
    rows = exchange(rows, "node").reshape(size, 2 * width)
    weights = (gate_w, up_w, across(gate_w), across(up_w))

    up_y, down_y = hop(rows, 1), hop(rows, -1)
    sums = gate_up([((rows,), 0), ((up_y,), chips - 1), ((down_y,), 1)], None, weights, idx)
    sums, down_w = lax.optimization_barrier((sums, w_down[0].T))
    down_other = across(down_w)
    for s in range(2, chips // 2):
        up_y, down_y = hop(up_y, 1), hop(down_y, -1)
        new = gate_up([((up_y,), chips - s), ((down_y,), s)], sums, weights, idx)
        down_y, sums = lax.optimization_barrier((down_y, sums))
        sums = new
    pairs = [(y, side) for y in range(chips) for side in range(2)]
    pairs = [(2 * y + side, 2 * ((y + 1 - 2 * side) % chips) + side) for y, side in pairs]
    sums, down_other = lax.optimization_barrier((sums, down_other))
    far = lax.ppermute(jnp.where(core[0] == 0, up_y, down_y), ("y", "core"), pairs)
    hidden = gate_up([((far,), chips // 2)], sums, weights, idx, last=chips)
    hidden = exchange(hidden, "y")
    out = down(core, hidden, down_w, down_other, half)
    back = exchange(out.reshape(2 * nodes, half, width), ("node", "core"))
    return combine(back.reshape(2 * nodes * half, width), pick, route_weight.T).T


def solution(mesh):
    shape = mesh.devices.shape
    split = Mesh(mesh.devices.reshape(shape[:2] + (shape[2] // 2, 2)), ("dp", "node", "y", "core"))
    rows, cols = ("dp", "node"), ("y", "core")
    return jax.shard_map(
        local,
        mesh=split,
        in_specs=(
            P(rows, cols),
            P(rows, None),
            P(rows, None),
            P("node", None, cols),
            P("node", None, cols),
            P("node", None, cols),
        ),
        out_specs=P(rows, cols),
        check_vma=False,
    )
```
